256 devices in a mesh: ctx: 16 (over z, core), head: 4 (over x), fsdp: 4 (over y).
Axes of the slice: x: 4, y: 4, z: 8, core: 2. Of those that a mesh axis runs over, the one named last changes fastest.
Arguments:
- ssm_input: bfloat16 [4, 4096, 4096], P('fsdp', 'ctx', 'head'), may hold values from -6 to 6
- input_map: bfloat16 [4, 4096, 128], P('fsdp', 'ctx'), may hold values from -6 to 6
- output_map: bfloat16 [4, 4096, 128], P('fsdp', 'ctx'), may hold values from -0.5 to 0.5
- step_raw: float32 [4, 64, 4096], P('fsdp', 'head', 'ctx'), may hold values from -2 to 12
- step_bias: float32 [64], P('head'), may hold values from -30 to -3
- decay_log: float32 [64], P('head'), may hold values from -0.7 to 0.7
- skip_gain: float32 [64], P('head'), may hold values from 0.3 to 1
- doc_lengths: int32 [4, 8], P('fsdp'), may hold values from 1 to 2048, 4096 in all within a row
- out_weight: bfloat16 [2048, 4096], P(('ctx', 'fsdp'), 'head'), may hold values from -0.09375 to 0.09375
- cotangent: bfloat16 [4, 4096, 2048], P('fsdp', 'ctx', 'head'), may hold values from -6 to 6
Outputs:
- input_grad: bfloat16 [4, 4096, 4096], P('fsdp', 'ctx', 'head')
- inmap_grad: bfloat16 [4, 4096, 128], P('fsdp', 'ctx')
- outmap_grad: bfloat16 [4, 4096, 128], P('fsdp', 'ctx')
- step_grad: float32 [4, 64, 4096], P('fsdp', 'head', 'ctx')
- weight_grad: float32 [2048, 4096], P(('ctx', 'fsdp'), 'head')
The draws below stay inside these ranges and needn't reach their ends.
Inputs may be any that keep to these rules, and one draw needn't show every extreme that they name: `doc_lengths`: row b lists the lengths of the 8 documents packed in order into sequence b, so that they sum to 4096.
All inputs are finite; a program needn't handle non-finite values.
Results may differ from the reference program's by a relative error of at most 0.015.
Values may be sent and summed in bfloat16 or wider, within the bound.
No kernel may reach another device: no remote copies, remote signals or barrier semaphores. Data moves between devices by JAX's collectives and lax.ppermute only.
A program may use at most 128 MiB of HBM per device.

```python
import math
import jax
import jax.numpy as jnp
import numpy as np
from jax import lax

D = 2048
HEADS = 64
HEAD_DIM = 64
STATE = 128
STRETCH = 256
DOCS = 8
TOKENS = 4096
BATCH = 4
INNER = 4096


def head_classes(key, share):
    return jax.random.uniform(jax.random.fold_in(key, 101), (HEADS,)) < share


def draw_step_bias(key, part):
    share = 0.5
    quick = head_classes(key, share)
    key = jax.random.fold_in(key, 1)
    jitter = jax.random.uniform(key, (HEADS,), jnp.float32, -0.3, 0.3)
    slow_level = math.log(0.4 / TOKENS)
    return jnp.where(quick, math.log(0.03), slow_level) + jitter


def draw_step_raw(key, part):
    share = 0.5
    quick = head_classes(key, share)
    key = jax.random.fold_in(key, 2)
    noise_key, spot_key = jax.random.split(key)
    noise = jnp.clip(0.4 * jax.random.normal(noise_key, (BATCH, HEADS, TOKENS), jnp.float32), -2.0, 2.0)
    spots = jax.random.randint(spot_key, (BATCH, 3), 0, TOKENS)
    hit = jnp.any(jnp.arange(TOKENS)[None, :, None] == spots[:, None, :], axis=2)
    lift = math.log(0.75 * TOKENS)
    boost = jnp.where(jnp.logical_and(hit[:, None, :], jnp.logical_not(quick)[None, :, None]), lift, 0.0)
    return (noise + boost).astype(jnp.float32)


def spiked(array, stream_key, source, target, parts, factor):
    def block_of(dim):
        return (jnp.arange(array.shape[dim]) // (array.shape[dim] // parts)).reshape((-1,) + (1,) * (array.ndim - 1 - dim))

    near = jax.random.permutation(stream_key, parts)[block_of(target)]
    second = (block_of(target) + parts // 2) % parts
    return jnp.where((block_of(source) == near) | (block_of(source) == second), factor * array, array)


def steps_of(own_key, shape, cuts, smallest, high):
    gain = 1.0
    for axis_at, parts in cuts:
        heights = jax.random.uniform(jax.random.fold_in(jax.random.fold_in(own_key, 6), axis_at), (parts,), jnp.float32, smallest / len(cuts), high / len(cuts))
        gain = gain * jnp.repeat(jnp.exp(heights), shape[axis_at] // parts).reshape((-1,) + (1,) * (len(shape) - 1 - axis_at))
    return gain


def split_up(number_of, total, most, skew):
    portions = [(1 << 20) // math.isqrt(rank ** skew) + 1 for rank in range(2, number_of + 1)]
    rest, holding = total - most - (number_of - 1), [1] * (number_of - 1)
    while rest > 0:
        candidates = [i for i in range(number_of - 1) if holding[i] < most]
        pool, budget = sum([portions[i] for i in candidates]), rest
        for i in candidates:
            extra = min(most - holding[i], max(1, budget * portions[i] // pool), rest)
            holding[i] = holding[i] + extra
            rest = rest - extra
    return np.array([most] + holding)


def uneven_parts(rng, amount, total, most, lean):
    if amount == 2:
        one = jax.random.randint(rng, (), max(1, total - most), min(most, total - 1) + 1)
        return jnp.stack([one, total - one])
    sizes = jnp.asarray(split_up(amount, total, most, lean), jnp.int32)
    pairs = (amount - 1) // 2
    giver, sink = sizes[1:1 + 2 * pairs:2], sizes[2:2 + 2 * pairs:2]
    room = jnp.minimum(giver - 1, most - sink)
    passed = jax.random.randint(jax.random.fold_in(rng, 1), (pairs,), 0, 1 << 20) % (room + 1)
    sizes = sizes.at[1:1 + 2 * pairs:2].set(giver - passed).at[2:2 + 2 * pairs:2].set(sink + passed)
    return sizes[jax.random.permutation(jax.random.fold_in(rng, 2), amount)]


def scatter_about(stream_key, shape, scale, limit, shards=(), kind=jnp.bfloat16):
    array = jax.random.normal(stream_key, shape, jnp.float32) * scale
    if len(shards) > 0:
        array = steps_of(stream_key, shape, shards, -0.22, 0.18) * array
    return jnp.clip(array, min=-limit, max=limit).astype(kind)


def gaussian_with(rng, dims, scale, bound, cuts, heavy, held_as=jnp.bfloat16):
    result = scale * jax.random.normal(rng, dims, jnp.float32)
    if cuts:
        result = result * steps_of(rng, dims, cuts, -0.22, 0.18)
    return jnp.clip(spiked(result, jax.random.fold_in(rng, 3), *heavy), -bound, bound).astype(held_as)


def setup_inputs(seed: int = 0) -> dict:
    keys = jax.random.split(jax.random.key(seed), 11)
    ssm_input = scatter_about(keys[0], (BATCH, TOKENS, INNER), 1.0, 6.0, ((0, 4), (1, 16), (2, 4)))
    input_map = scatter_about(keys[1], (BATCH, TOKENS, STATE), 1.0, 6.0, ((0, 4), (1, 16)))
    output_map = scatter_about(keys[2], (BATCH, TOKENS, STATE), STATE ** -0.5, 0.5, ((0, 4), (1, 16)))
    step_raw = draw_step_raw(jax.random.fold_in(keys[10], 71), 0)
    step_bias = draw_step_bias(jax.random.fold_in(keys[10], 71), 0)
    decay_log = jnp.clip(jax.random.uniform(keys[5], (HEADS,), jnp.float32, -0.7, 0.7) * steps_of(keys[5], (HEADS,), ((0, 4),), -0.4, 0.0), -0.7, 0.7)
    skip_gain = jnp.clip(0.3 + 0.7 * jax.random.uniform(keys[6], (HEADS,), jnp.float32) ** steps_of(keys[6], (HEADS,), ((0, 4),), -0.2, 0.2), 0.3, 1.0)
    doc_lengths = jax.vmap(lambda own: uneven_parts(own, DOCS, TOKENS, TOKENS // 2, 2))(jax.random.split(keys[7], BATCH)).reshape((BATCH, DOCS)).astype(jnp.int32)
    out_weight = scatter_about(keys[8], (D, INNER), INNER ** -0.5, 0.09375, ((0, 64), (1, 4)))
    cotangent = gaussian_with(keys[9], (BATCH, TOKENS, D), 1.0, 6.0, ((0, 4), (1, 16), (2, 4)), (1, 2, 16, 2.0))
    return dict(ssm_input=ssm_input, input_map=input_map, output_map=output_map, step_raw=step_raw, step_bias=step_bias, decay_log=decay_log, skip_gain=skip_gain, doc_lengths=doc_lengths, out_weight=out_weight, cotangent=cotangent)


precise = lax.Precision.HIGHEST

def block_maker(decay_rate, skip_gain):

    def advance(state_prev, block):
        block_x, block_b, block_c, block_dt, block_starts = block
        size_k = block_x.shape[0]
        running = jnp.cumsum(block_dt * decay_rate[:, None], axis=1)
        segment = jnp.cumsum(block_starts)
        order_ok = jnp.arange(size_k)[:, None] >= jnp.arange(size_k)[None, :]
        linked = jnp.logical_and(order_ok, segment[:, None] == segment[None, :])[None]
        spread = running[:, :, None] - running[:, None, :]
        decay = jnp.where(linked, jnp.exp(jnp.where(linked, spread, 0.0)), 0.0)
        scores = jnp.dot(block_c, block_b.T, precision=precise)
        mixing = decay * scores[None] * block_dt[:, None, :]
        inner = jnp.einsum('htu,uhp->thp', mixing, block_x, precision=precise)
        leading = (segment == 0).astype(block_x.dtype)
        reach = leading[None, :] * jnp.exp(running)
        carried = jnp.einsum('tn,hpn->thp', block_c, state_prev, precision=precise) * reach.T[:, :, None]
        output = inner + carried + skip_gain[None, :, None] * block_x
        trailing = (segment == segment[-1]).astype(block_x.dtype)
        ending = trailing[None, :] * jnp.exp(running[:, -1:] - running) * block_dt
        through = (segment[-1] == 0).astype(block_x.dtype) * jnp.exp(running[:, -1])
        state_next = through[:, None, None] * state_prev + jnp.einsum('hu,uhp,un->hpn', ending, block_x, block_b, precision=precise)
        return (state_next, output)
    return jax.checkpoint(advance)

def run_slab(x_part, b_part, c_part, raw_part, step_bias, decay_rate, skip_gain, doc_starts, state_start):
    head_count = raw_part.shape[0]
    length = x_part.shape[0]
    blocks = length // STRETCH
    step_size = jax.nn.softplus(raw_part + step_bias[:, None])
    block_x = x_part.reshape(blocks, STRETCH, head_count, -1)
    block_b = b_part.reshape(blocks, STRETCH, -1)
    block_c = c_part.reshape(blocks, STRETCH, -1)
    block_dt = step_size.reshape(head_count, blocks, STRETCH).transpose(1, 0, 2)
    block_starts = doc_starts.reshape(blocks, STRETCH)
    state_end, outputs = lax.scan(block_maker(decay_rate, skip_gain), state_start, (block_x, block_b, block_c, block_dt, block_starts))
    return (outputs.reshape(length, -1), state_end)

def reference(ssm_input, input_map, output_map, step_raw, step_bias, decay_log, skip_gain, doc_lengths, out_weight, cotangent):
    decay_rate = -jnp.exp(decay_log)
    norm_scale = 1.0 / math.sqrt(BATCH * TOKENS)

    def one_sequence(inputs):
        seq_x, seq_b, seq_c, seq_raw, seq_lengths, seq_cot = inputs
        firsts = jnp.cumsum(seq_lengths) - seq_lengths
        positions = jnp.arange(TOKENS).astype(jnp.int32)
        doc_starts = jnp.any(positions[:, None] == firsts[None, :], axis=1).astype(jnp.int32)
        grad_out = jnp.dot(seq_cot, out_weight, preferred_element_type=jnp.float32)
        state_zero = jnp.zeros((HEADS, HEAD_DIM, STATE), jnp.float32)

        def forward(x_part, b_part, c_part, raw_part):
            return run_slab(x_part, b_part, c_part, raw_part, step_bias, decay_rate, skip_gain, doc_starts, state_zero)[0]
        ssm_out, pullback = jax.vjp(forward, seq_x.astype(jnp.float32), seq_b.astype(jnp.float32), seq_c.astype(jnp.float32), seq_raw)
        grad_x, grad_b, grad_c, grad_raw = pullback(grad_out)
        rounded = ssm_out.astype(jnp.bfloat16)
        weight_term = lax.dot_general(seq_cot, rounded, (((0,), (0,)), ((), ())), preferred_element_type=jnp.float32)
        return (grad_x.astype(jnp.bfloat16), grad_b.astype(jnp.bfloat16), grad_c.astype(jnp.bfloat16), grad_raw, weight_term)
    results = lax.map(one_sequence, (ssm_input, input_map, output_map, step_raw, doc_lengths, cotangent))
    weight_grad = lax.optimization_barrier(jnp.sum(results[4], axis=0)) * norm_scale
    return (results[0], results[1], results[2], results[3], weight_grad)
```

```python
import functools
import math

import jax
import jax.numpy as jnp
from jax import lax
from jax.experimental import pallas as pl
from jax.experimental.pallas import tpu as pltpu
from jax.sharding import Mesh, PartitionSpec as P

F32 = jnp.float32
BF16 = jnp.bfloat16
LOG2E = 1.4426950408889634
HIGH = lax.Precision.HIGHEST

T = 256
H = 16
HD = 64
N = 128
W = H * HD
FC = 1024
Z, Y, X = 8, 4, 4
PAY = HD + 16

CUM, CUMDT, REACH, END, DT, SIG, THRU, SEG = range(0, 128, 16)


def nt(a, b, **kw):
    return lax.dot_general(a, b, (((1,), (1,)), ((), ())), preferred_element_type=F32, **kw)


def nn(a, b, **kw):
    return lax.dot_general(a, b, (((1,), (0,)), ((), ())), preferred_element_type=F32, **kw)


def tn(a, b, **kw):
    return lax.dot_general(a, b, (((0,), (0,)), ((), ())), preferred_element_type=F32, **kw)


def call(body, outs, ins, flops=1e8, smem=(), scratch=(), limit=40):
    shapes = [jax.ShapeDtypeStruct(s, d) for s, d in outs]
    size = sum(a.size * a.dtype.itemsize for a in ins)
    size += sum(math.prod(s) * jnp.dtype(d).itemsize for s, d in outs)
    specs = [
        pl.BlockSpec(memory_space=pltpu.SMEM if i in smem else pltpu.VMEM)
        for i in range(len(ins))
    ]
    return pl.pallas_call(
        body,
        out_shape=shapes,
        in_specs=specs,
        out_specs=[pl.BlockSpec(memory_space=pltpu.VMEM)] * len(shapes),
        scratch_shapes=list(scratch),
        compiler_params=pltpu.CompilerParams(vmem_limit_bytes=limit << 20),
        cost_estimate=pl.CostEstimate(
            flops=int(flops), bytes_accessed=int(size), transcendentals=0
        ),
    )(*ins)


def pair_columns(vt_ref, group, j):
    low = lax.broadcasted_iota(jnp.int32, (T, 128), 1) < HD
    a = vt_ref[:, group + 2 * j : group + 2 * j + 1]
    b = vt_ref[:, group + 2 * j + 1 : group + 2 * j + 2]
    return jnp.where(low, a, b)


def pair_scalars(ref, j):
    low = lax.broadcasted_iota(jnp.int32, (1, 128), 1) < HD
    return jnp.where(low, ref[2 * j], ref[2 * j + 1])


def halves(v):
    low = (lax.broadcasted_iota(jnp.int32, (1, 128), 1) < HD).astype(v.dtype)
    return v * low, v * (1 - low)


def join_rows(idx, *refs):
    out = refs[-1]
    z = idx[0]
    for d in range(Z):
        out[(z - d + Z) % Z] = refs[d][...]


def join_cot(idx, here, left, right, far_a, far_b, own, send):
    c, x = idx[1], idx[2]
    half = T // 2
    for d, parts in (
        (0, ((here, 0, T),)),
        (1, ((left, 0, T),)),
        (2, ((far_a, 0, half), (far_b, half, half))),
        (3, ((right, 0, T),)),
    ):
        base = ((x - d + X) % X) * 256
        for k in range(2):
            to = pl.ds(pl.multiple_of(base + k * 128, 128), 128)
            at = pl.ds(pl.multiple_of(k * 256 + c * 128, 128), 128)
            other = pl.ds(pl.multiple_of(k * 256 + (1 - c) * 128, 128), 128)
            for ref, start, size in parts:
                own[start : start + size, to] = ref[:, at]
                send[start : start + size, to] = ref[:, other]


def local_state(idx, lens, raw, bias, dlog, x, b, pay, vecs, vecst):
    base = (idx[0] * 2 + idx[1]) * T
    v = raw[...] + bias[...]
    dt = jnp.maximum(v, 0.0) + jnp.log1p(jnp.exp(-jnp.abs(v)))
    a = -jnp.exp(dlog[...]) * dt * LOG2E
    row = lax.broadcasted_iota(jnp.int32, (T, T), 0)
    col = lax.broadcasted_iota(jnp.int32, (T, T), 1)
    cum = nn(a, (row <= col).astype(F32), precision=HIGH)
    cumdt = cum - jnp.log(dt) * LOG2E
    pos = base + lax.broadcasted_iota(jnp.int32, (H, T), 1)
    seg = jnp.zeros((H, T), F32)
    last = jnp.float32(0)
    first = jnp.int32(0)
    for k in range(8):
        here = first >= base
        seg = seg + jnp.where(jnp.logical_and(here, pos >= first), 1.0, 0.0)
        last = last + jnp.where(jnp.logical_and(here, first < base + T), 1.0, 0.0)
        first = first + lens[0, k]
    end = jnp.where(seg == last, jnp.exp2(cum[:, T - 1 :] - cumdt), 0.0)
    reach = jnp.where(seg == 0.0, jnp.exp2(cum), 0.0)
    thru = jnp.where(last == 0.0, jnp.exp2(cum[:, T - 1 :]), 0.0)
    thru = jnp.broadcast_to(thru, (H, T))
    for at, value in (
        (CUM, cum),
        (CUMDT, cumdt),
        (REACH, reach),
        (END, end),
        (DT, dt),
        (SIG, jax.nn.sigmoid(v)),
        (THRU, thru),
        (SEG, seg),
    ):
        vecs[at : at + H, :] = value
    vecst[...] = vecs[...].T
    for j in range(H // 2):
        xs = x[:, j * 128 : (j + 1) * 128].astype(F32) * pair_columns(vecst, END, j)
        s = tn(xs.astype(BF16), b[...])
        pay[2 * j, 0:HD, :] = s[0:HD].astype(BF16)
        pay[2 * j + 1, 0:HD, :] = s[HD:].astype(BF16)
    hi = thru.astype(BF16)
    lo = (thru - hi.astype(F32)).astype(BF16)
    for h in range(H):
        pay[h, HD : HD + 8, :] = jnp.broadcast_to(hi[h : h + 1, 0:128].astype(F32), (8, 128)).astype(BF16)
        pay[h, HD + 8 :, :] = jnp.broadcast_to(lo[h : h + 1, 0:128].astype(F32), (8, 128)).astype(BF16)


def decay_of(block):
    tail = block[HD:, :].astype(F32)
    return tail[0:1] + tail[8:9]


def chip_state(idx, mine, theirs, out):
    c = idx[1]
    for k in range(8):
        m, t = mine[c * 8 + k], theirs[c * 8 + k]
        a = jnp.where(c == 0, m.astype(F32), t.astype(F32))
        b = jnp.where(c == 0, t.astype(F32), m.astype(F32))
        ta = a[HD : HD + 1] + a[HD + 8 : HD + 9]
        tb = b[HD : HD + 1] + b[HD + 8 : HD + 9]
        out[k, 0:HD, :] = (tb * a[0:HD] + b[0:HD]).astype(BF16)
        t = jnp.broadcast_to(ta * tb, (8, 128))
        hi = t.astype(BF16).astype(F32)
        out[k, HD:, :] = jnp.concatenate([hi, t - hi], axis=0).astype(BF16)


def scan_state(idx, *refs):
    z = idx[0]
    ins, out, decays = refs[: Z - 1], refs[Z - 1], refs[Z]
    for k in range(8):
        state = jnp.zeros((HD, N), F32)
        through = jnp.ones((1, N), F32)
        for d in range(1, Z):
            block = ins[d - 1][k].astype(F32)
            decay = block[HD : HD + 1] + block[HD + 8 : HD + 9]
            state = state + jnp.where(d <= z, through, 0.0) * block[0:HD]
            through = through * decay
            decays[d, k : k + 1, :] = decay
        out[k] = state.astype(BF16)


def chip_adjoint(idx, mine, theirs, pay_mine, pay_theirs, out):
    c = idx[1]
    for k in range(8):
        h = c * 8 + k
        m, t = mine[h].astype(F32), theirs[h].astype(F32)
        ta = jnp.where(c == 0, decay_of(pay_mine[h]), decay_of(pay_theirs[h]))
        a = jnp.where(c == 0, m, t)
        b = jnp.where(c == 0, t, m)
        out[k] = (a + ta * b).astype(BF16)


def scan_adjoint(idx, decays, *refs):
    z = idx[0]
    ins, out = refs[: Z - 1], refs[Z - 1]
    for k in range(8):
        state = jnp.zeros((HD, N), F32)
        through = jnp.ones((1, N), F32)
        for d in range(1, Z):
            block = ins[d - 1][k].astype(F32)
            state = state + jnp.where(z + d < Z, through, 0.0) * block
            through = through * decays[Z - d, k : k + 1, :]
        out[k] = state.astype(BF16)


def place_states(idx, mine, theirs, local, pay, out, needs):
    c = idx[1]
    for k in range(8):
        for group, ref in ((c * 8, mine), (8 - c * 8, theirs)):
            h = group + k
            e = ref[k].astype(F32)
            past = decay_of(pay[h]) * e + local[h, 0:HD, :].astype(F32)
            at = pl.multiple_of(h * HD, HD)
            out[pl.ds(at, HD), :] = jnp.where(c == needs, past, e).astype(BF16)


def causal(vecs, vecst, transposed):
    row = lax.broadcasted_iota(jnp.int32, (T, T), 0)
    col = lax.broadcasted_iota(jnp.int32, (T, T), 1)
    order = row <= col if transposed else row >= col
    same = vecst[:, SEG : SEG + 1] == vecs[SEG : SEG + 1, :]
    return jnp.where(jnp.logical_and(order, same), 0.0, -1e30)


def inner_part(vecs, vecst, x, b, c, out):
    scores = nt(c[...], b[...])
    mask = causal(vecs, vecst, False)
    for j in range(H // 2):
        xs = halves(x[:, j * 128 : (j + 1) * 128])
        acc = None
        for k in range(2):
            h = 2 * j + k
            decay = jnp.exp2(
                vecst[:, CUM + h : CUM + h + 1] - vecs[CUMDT + h : CUMDT + h + 1, :] + mask
            )
            term = nn((decay * scores).astype(BF16), xs[k])
            acc = term if acc is None else acc + term
        out[:, j * 128 : (j + 1) * 128] = acc


def forward_out(idx, skip, vecst, x, c, inner, mine, theirs, pay, yy, rounded, state):
    place_states(idx, mine, theirs, pay, pay, state, 1)
    for j in range(H // 2):
        cols = slice(j * 128, (j + 1) * 128)
        carried = nt(c[...], state[j * 128 : (j + 1) * 128, :])
        y = inner[:, cols] + carried * pair_columns(vecst, REACH, j)
        yy[:, cols] = y
        rounded[:, cols] = (y + pair_scalars(skip, j) * x[:, cols].astype(F32)).astype(BF16)


def weight_part(idx, cot, cot_t, mine, theirs, *refs):
    y = idx[3]
    outs, buf = refs[:7], refs[7]
    p0, p1a, p1b, p2a, p2b, p3a, p3b = outs
    for n in range(4):
        cols = slice(n * 256, (n + 1) * 256)
        r = tn(cot[...], mine[:, cols]) + tn(cot_t[...], theirs[:, cols])
        buf[:, :, :, cols] = r.reshape(Z, Y, 32, 256).astype(BF16)
    p0[...] = buf[:, y]
    p1a[...] = buf[:, (y + 1) % Y, :, 0:512]
    p1b[...] = buf[:, (y + 1) % Y, :, 512:]
    p2a[...] = buf[:, (y + 2) % Y, :, 0:512]
    p2b[...] = buf[:, (y + 2) % Y, :, 512:]
    p3a[...] = buf[:, (y + 3) % Y, :, 0:512]
    p3b[...] = buf[:, (y + 3) % Y, :, 512:]


def sum_rows(idx, p0, la, lb, ra, rb, *outs):
    z = idx[0]
    for d in range(Z):
        k = (z + d) % Z
        for cols, left, right in ((slice(0, 512), la, ra), (slice(512, 1024), lb, rb)):
            s = p0[k, :, cols].astype(F32) + left[k].astype(F32) + right[k].astype(F32)
            outs[d][:, cols] = s.astype(BF16)


def sum_blocks(*refs):
    s = refs[0][...].astype(F32)
    for ref in refs[1:-1]:
        s = s + ref[...].astype(F32)
    refs[-1][...] = s * (1.0 / 128.0)


def out_grad(idx, cot, cot_t, here, left, right, far_a, far_b, own, send, weights):
    y = idx[3]
    weights[:, y] = here[...]
    weights[:, (y + 3) % Y] = left[...]
    weights[:, (y + 1) % Y] = right[...]
    weights[0:4, (y + 2) % Y] = far_a[...]
    weights[4:8, (y + 2) % Y] = far_b[...]
    for n in range(4):
        cols = slice(n * 256, (n + 1) * 256)
        w = weights[:, :, :, cols].reshape(FC, 256)
        send[:, cols] = nn(cot_t[...], w).astype(BF16)
        own[:, cols] = nn(cot[...], w)


def local_adjoint(vecst, own, got, c, g, adj):
    for j in range(H // 2):
        cols = slice(j * 128, (j + 1) * 128)
        gj = (own[:, cols] + got[:, cols].astype(F32)).astype(BF16)
        g[:, cols] = gj
        gr = (gj.astype(F32) * pair_columns(vecst, REACH, j)).astype(BF16)
        s = tn(gr, c[...])
        adj[2 * j] = s[0:HD].astype(BF16)
        adj[2 * j + 1] = s[HD:].astype(BF16)


def inner_grads(vecs, vecst, x, b, c, g, state, dx, dc, db):
    scores = nt(b[...], c[...])
    mask = causal(vecs, vecst, True)
    dscores = jnp.zeros((T, T), F32)
    dstate = jnp.zeros((T, N), F32)
    for j in range(H // 2):
        cols = slice(j * 128, (j + 1) * 128)
        gj = g[:, cols]
        gs, xs = halves(gj), halves(x[:, cols])
        acc = None
        for k in range(2):
            h = 2 * j + k
            decay = jnp.exp2(
                vecs[CUM + h : CUM + h + 1, :] - vecst[:, CUMDT + h : CUMDT + h + 1] + mask
            )
            term = nn((decay * scores).astype(BF16), gs[k])
            acc = term if acc is None else acc + term
            dscores = dscores + nt(xs[k], gj) * decay
        dx[:, cols] = acc
        gr = (gj.astype(F32) * pair_columns(vecst, REACH, j)).astype(BF16)
        dstate = dstate + nn(gr, state[j * 128 : (j + 1) * 128, :])
    ds = dscores.astype(BF16)
    db[...] = nn(ds, c[...])
    dc[...] = tn(ds, b[...]) + dstate


def two_part(ones, v):
    hi = v.astype(BF16)
    lo = (v - hi.astype(F32)).astype(BF16)
    return nt(ones, hi) + nt(ones, lo)


def final_grads(
    idx, skip, vecs, vecst, dlog, x, b, g, yy, dxm, dbp, state, mine, theirs, adjt, pay,
    dc, dx, maps, dstep, adj, flow, direct,
):
    place_states(idx, mine, theirs, adjt, pay, adj, 0)
    dbs = dbp[...]
    ends = []
    for j in range(H // 2):
        cols = slice(j * 128, (j + 1) * 128)
        rows = slice(j * 128, (j + 1) * 128)
        end = pair_columns(vecst, END, j)
        xj = x[:, cols].astype(F32)
        gj = g[:, cols].astype(F32)
        dxe = end * nt(b[...], adj[rows, :])
        dxx = dxm[:, cols] + dxe
        dx[:, cols] = (dxx + pair_scalars(skip, j) * gj).astype(BF16)
        dbs = dbs + nn((xj * end).astype(BF16), adj[rows, :])
        prod = xj * dxx
        direct[:, cols] = prod
        flow[:, cols] = gj * yy[:, cols] - prod
        ends.append(jnp.sum(xj * dxe, axis=0, keepdims=True))
    maps[:, 0:N] = dbs.astype(BF16)
    maps[:, N:] = dc[...].astype(BF16)
    head = lax.broadcasted_iota(jnp.int32, (H, W), 0)
    lane = lax.broadcasted_iota(jnp.int32, (H, W), 1)
    member = jnp.logical_and(lane >= head * HD, lane < head * HD + HD)
    ones = member.astype(BF16)
    dcum = two_part(ones, flow[...])
    ddt = two_part(ones, direct[...])
    total = jnp.sum(jnp.where(member, jnp.concatenate(ends, axis=1), 0.0), axis=1, keepdims=True)
    cross = jnp.sum(adj[...].astype(F32) * state[...].astype(F32), axis=1, keepdims=True)
    hi = cross.astype(BF16).astype(F32)
    cross = nn(ones, jnp.broadcast_to(hi, (W, 128)).astype(BF16)) + nn(
        ones, jnp.broadcast_to(cross - hi, (W, 128)).astype(BF16)
    )
    row = lax.broadcasted_iota(jnp.int32, (T, T), 0)
    col = lax.broadcasted_iota(jnp.int32, (T, T), 1)
    da = nn(dcum, (row >= col).astype(F32), precision=HIGH)
    da = da + total + vecs[THRU : THRU + H, 0:1] * cross[:, 0:1]
    ddt = ddt / vecs[DT : DT + H, :] - jnp.exp(dlog[...]) * da
    dstep[...] = ddt * vecs[SIG : SIG + H, :]


def sum_maps(*refs):
    s = sum(r[...].astype(F32) for r in refs[:-2]).astype(BF16)
    refs[-2][...] = s[:, 0:N]
    refs[-1][...] = s[:, N:]


def shift(v, axis, count, d):
    return lax.ppermute(v, axis, [(i, (i + d) % count) for i in range(count)])


def swap(v):
    return lax.ppermute(v, "core", [(0, 1), (1, 0)])


def spread(blocks):
    return [blocks[0]] + [shift(blocks[d], "z", Z, d) for d in range(1, Z)]


def ring(block):
    rights, lefts = [block], [block]
    for k in range(4):
        rights.append(shift(rights[-1], "z", Z, 1))
        if k < 3:
            lefts.append(shift(lefts[-1], "z", Z, -1))
    return rights + lefts[:0:-1]


def both_ways(v, axis, count):
    left, right = shift(v, axis, count, 1), shift(v, axis, count, -1)
    half = v.shape[0] // 2
    return v, left, right, shift(left[:half], axis, count, 1), shift(right[half:], axis, count, -1)


def on_device(
    ssm_input, input_map, output_map, step_raw, step_bias, decay_log, skip_gain, doc_lengths,
    out_weight, cotangent,
):
    x, b, c = ssm_input[0], input_map[0], output_map[0]
    raw, bias, dlog = step_raw[0], step_bias[:, None], decay_log[:, None]
    idx = jnp.stack([lax.axis_index(a) for a in ("z", "core", "head", "fsdp")]).astype(jnp.int32)

    cot, cot_send = call(
        join_cot,
        [((T, FC), BF16)] * 2,
        [idx, *both_ways(cotangent[0], "head", X)],
        smem=(0,),
    )
    cot_t = swap(cot_send)

    (bundle,) = call(
        join_rows, [((Z, 32, W), BF16)], [idx, *ring(out_weight)], smem=(0,)
    )
    bundles = both_ways(bundle, "fsdp", Y)

    pay, vecs, vecst = call(
        local_state,
        [((H, PAY, N), BF16), ((128, T), F32), ((T, 128), F32)],
        [idx, doc_lengths, raw, bias, dlog, x, b],
        smem=(0, 1),
    )
    pay_t = swap(pay)
    (block,) = call(chip_state, [((8, PAY, N), BF16)], [idx, pay, pay_t], smem=(0,))
    mine, decays = call(
        scan_state,
        [((8, HD, N), BF16), ((Z, 8, N), F32)],
        [idx, *ring(block)[1:]],
        smem=(0,),
    )
    theirs = swap(mine)
    (inner,) = call(inner_part, [((T, W), F32)], [vecs, vecst, x, b, c], flops=5e9)
    yy, rounded, state = call(
        forward_out,
        [((T, W), F32), ((T, W), BF16), ((W, N), BF16)],
        [idx, skip_gain, vecst, x, c, inner, mine, theirs, pay_t],
        smem=(0, 1),
    )

    rounded_t = swap(rounded)
    p0, p1a, p1b, p2a, p2b, p3a, p3b = call(
        weight_part,
        [((Z, 32, W), BF16)] + [((Z, 32, W // 2), BF16)] * 6,
        [idx, cot, cot_t, rounded, rounded_t],
        flops=2e9,
        smem=(0,),
        scratch=[pltpu.VMEM((Z, Y, 32, W), BF16)],
    )
    via_a, via_b = shift(p2a, "fsdp", Y, 1), shift(p2b, "fsdp", Y, -1)
    lb, ra = shift(p1b, "fsdp", Y, 1), shift(p3a, "fsdp", Y, -1)
    add = lambda u, v: (u.astype(F32) + v.astype(F32)).astype(BF16)
    la, rb = shift(add(p1a, via_a), "fsdp", Y, 1), shift(add(p3b, via_b), "fsdp", Y, -1)
    rows = call(
        sum_rows, [((32, W), BF16)] * Z, [idx, p0, la, lb, ra, rb], smem=(0,)
    )
    (weight_grad,) = call(sum_blocks, [((32, W), F32)], spread(rows))

    part, part_t = call(
        out_grad,
        [((T, W), F32), ((T, W), BF16)],
        [idx, cot, cot_t, *bundles],
        flops=2e9,
        smem=(0,),
        scratch=[pltpu.VMEM((Z, Y, 32, W), BF16)],
    )
    g, adj = call(
        local_adjoint, [((T, W), BF16), ((H, HD, N), BF16)], [vecst, part, swap(part_t), c]
    )
    adj_t = swap(adj)
    (block,) = call(
        chip_adjoint, [((8, HD, N), BF16)], [idx, adj, adj_t, pay, pay_t], smem=(0,)
    )
    (mine,) = call(
        scan_adjoint,
        [((8, HD, N), BF16)],
        [idx, decays, *ring(block)[:0:-1]],
        smem=(0,),
    )
    theirs = swap(mine)
    dxm, dc, dbp = call(
        inner_grads,
        [((T, W), F32), ((T, N), F32), ((T, N), F32)],
        [vecs, vecst, x, b, c, g, state],
        flops=5e9,
    )
    dx, maps, dstep = call(
        final_grads,
        [((T, W), BF16), ((T, 2 * N), BF16), ((H, T), F32)],
        [idx, skip_gain, vecs, vecst, dlog, x, b, g, yy, dxm, dbp, state, mine, theirs, adj_t, pay_t, dc],
        smem=(0, 1),
        scratch=[pltpu.VMEM((W, N), BF16), pltpu.VMEM((T, W), F32), pltpu.VMEM((T, W), F32)],
    )
    db, dc = call(
        sum_maps,
        [((T, N), BF16)] * 2,
        [maps] + [shift(maps, "head", X, d) for d in (1, 2, 3)],
    )
    return dx[None], db[None], dc[None], dstep[None], weight_grad


def solution(mesh):
    inner = Mesh(mesh.devices.reshape(Z, 2, X, Y), ("z", "core", "head", "fsdp"))
    ctx = ("z", "core")
    features = ("z", "core", "fsdp")
    return jax.shard_map(
        on_device,
        mesh=inner,
        in_specs=(
            P("fsdp", ctx, "head"),
            P("fsdp", ctx, None),
            P("fsdp", ctx, None),
            P("fsdp", "head", ctx),
            P("head"),
            P("head"),
            P("head"),
            P("fsdp", None),
            P(features, "head"),
            P("fsdp", ctx, "head"),
        ),
        out_specs=(
            P("fsdp", ctx, "head"),
            P("fsdp", ctx, None),
            P("fsdp", ctx, None),
            P("fsdp", "head", ctx),
            P(features, "head"),
        ),
        check_vma=False,
    )
```

```python
import functools
import math

import jax
import jax.numpy as jnp
from jax import lax
from jax.experimental import pallas as pl
from jax.experimental.pallas import tpu as pltpu
from jax.sharding import Mesh, PartitionSpec as P

F32 = jnp.float32
BF16 = jnp.bfloat16
LOG2E = 1.4426950408889634
HIGH = lax.Precision.HIGHEST

T = 256
H = 16
HD = 64
N = 128
W = H * HD
FC = 1024
Z, Y, X = 8, 4, 4
PAY = HD + 16

CUM, CUMDT, REACH, END, DT, SIG, THRU, SEG = range(0, 128, 16)


def nt(a, b, **kw):
    return lax.dot_general(a, b, (((1,), (1,)), ((), ())), preferred_element_type=F32, **kw)


def nn(a, b, **kw):
    return lax.dot_general(a, b, (((1,), (0,)), ((), ())), preferred_element_type=F32, **kw)


def tn(a, b, **kw):
    return lax.dot_general(a, b, (((0,), (0,)), ((), ())), preferred_element_type=F32, **kw)


def call(body, outs, ins, smem=(), hbm=(), scratch=(), limit=40):
    shapes = [jax.ShapeDtypeStruct(s, d) for s, d in outs]
    specs = [
        pl.BlockSpec(
            memory_space=pltpu.SMEM if i in smem else pltpu.HBM if i in hbm else pltpu.VMEM
        )
        for i in range(len(ins))
    ]
    return pl.pallas_call(
        body,
        out_shape=shapes,
        in_specs=specs,
        out_specs=[pl.BlockSpec(memory_space=pltpu.VMEM)] * len(shapes),
        scratch_shapes=list(scratch),
        compiler_params=pltpu.CompilerParams(vmem_limit_bytes=limit << 20),
        cost_estimate=pl.CostEstimate(
            flops=1, bytes_accessed=1, transcendentals=0
        ),
    )(*ins)


def pair_columns(vt_ref, group, j):
    low = lax.broadcasted_iota(jnp.int32, (T, 128), 1) < HD
    a = vt_ref[:, group + 2 * j : group + 2 * j + 1]
    b = vt_ref[:, group + 2 * j + 1 : group + 2 * j + 2]
    return jnp.where(low, a, b)


def pair_scalars(ref, j):
    low = lax.broadcasted_iota(jnp.int32, (1, 128), 1) < HD
    return jnp.where(low, ref[2 * j], ref[2 * j + 1])


def halves(v):
    low = (lax.broadcasted_iota(jnp.int32, (1, 128), 1) < HD).astype(v.dtype)
    return v * low, v * (1 - low)


def stack_rows(*refs):
    for i, ref in enumerate(refs[:-1]):
        refs[-1][i] = ref[...]


def join_cot(idx, here, left, right, far, own, send):
    c, x = idx[1], idx[2]
    for d, ref in enumerate((here, left, far, right)):
        base = ((x - d + X) % X) * 256
        for k in range(2):
            to = pl.ds(pl.multiple_of(base + k * 128, 128), 128)
            at = pl.ds(pl.multiple_of(k * 256 + c * 128, 128), 128)
            other = pl.ds(pl.multiple_of(k * 256 + (1 - c) * 128, 128), 128)
            own[:, to] = ref[:, at]
            send[:, to] = ref[:, other]


def head_column(ref):
    head = lax.broadcasted_iota(jnp.int32, (H, 1), 0)
    out = jnp.zeros((H, 1), F32)
    for h in range(H):
        out = jnp.where(head == h, ref[h], out)
    return out


def local_state(
    idx, lens, bias, dlog, raw_hbm, x_hbm, b_hbm, pay, vecs, vecst, raw, x, b, sems
):
    copies = [
        pltpu.make_async_copy(src, dst, sems.at[i])
        for i, (src, dst) in enumerate(((raw_hbm, raw), (x_hbm, x), (b_hbm, b)))
    ]
    for copy in copies:
        copy.start()
    base = (idx[0] * 2 + idx[1]) * T
    copies[0].wait()
    v = raw[...] + head_column(bias)
    dt = jnp.maximum(v, 0.0) + jnp.log1p(jnp.exp(-jnp.abs(v)))
    a = -jnp.exp(head_column(dlog)) * dt * LOG2E
    row = lax.broadcasted_iota(jnp.int32, (T, T), 0)
    col = lax.broadcasted_iota(jnp.int32, (T, T), 1)
    cum = nn(a, (row <= col).astype(F32), precision=HIGH)
    cumdt = cum - jnp.log(dt) * LOG2E
    pos = base + lax.broadcasted_iota(jnp.int32, (H, T), 1)
    seg = jnp.zeros((H, T), F32)
    last = jnp.float32(0)
    first = jnp.int32(0)
    for k in range(8):
        here = first >= base
        seg = seg + jnp.where(jnp.logical_and(here, pos >= first), 1.0, 0.0)
        last = last + jnp.where(jnp.logical_and(here, first < base + T), 1.0, 0.0)
        first = first + lens[0, k]
    end = jnp.where(seg == last, jnp.exp2(cum[:, T - 1 :] - cumdt), 0.0)
    reach = jnp.where(seg == 0.0, jnp.exp2(cum), 0.0)
    thru = jnp.where(last == 0.0, jnp.exp2(cum[:, T - 1 :]), 0.0)
    thru = jnp.broadcast_to(thru, (H, T))
    for at, value in (
        (CUM, cum),
        (CUMDT, cumdt),
        (REACH, reach),
        (END, end),
        (DT, dt),
        (SIG, jax.nn.sigmoid(v)),
        (THRU, thru),
        (SEG, seg),
    ):
        vecs[at : at + H, :] = value
    vecst[...] = vecs[...].T
    copies[1].wait()
    copies[2].wait()
    for j in range(H // 2):
        xs = x[:, j * 128 : (j + 1) * 128].astype(F32) * pair_columns(vecst, END, j)
        s = tn(xs.astype(BF16), b[...])
        pay[2 * j, 0:HD, :] = s[0:HD].astype(BF16)
        pay[2 * j + 1, 0:HD, :] = s[HD:].astype(BF16)
    hi = thru.astype(BF16)
    lo = (thru - hi.astype(F32)).astype(BF16)
    for h in range(H):
        pay[h, HD : HD + 8, :] = jnp.broadcast_to(hi[h : h + 1, 0:128].astype(F32), (8, 128)).astype(BF16)
        pay[h, HD + 8 :, :] = jnp.broadcast_to(lo[h : h + 1, 0:128].astype(F32), (8, 128)).astype(BF16)


def decay_of(block):
    tail = block[HD:, :].astype(F32)
    return tail[0:1] + tail[8:9]


def chip_state(idx, mine, theirs, out):
    c = idx[1]
    for k in range(8):
        m, t = mine[c * 8 + k], theirs[c * 8 + k]
        a = jnp.where(c == 0, m.astype(F32), t.astype(F32))
        b = jnp.where(c == 0, t.astype(F32), m.astype(F32))
        ta = a[HD : HD + 1] + a[HD + 8 : HD + 9]
        tb = b[HD : HD + 1] + b[HD + 8 : HD + 9]
        out[k, 0:HD, :] = (tb * a[0:HD] + b[0:HD]).astype(BF16)
        t = jnp.broadcast_to(ta * tb, (8, 128))
        hi = t.astype(BF16).astype(F32)
        out[k, HD:, :] = jnp.concatenate([hi, t - hi], axis=0).astype(BF16)


def merge_state(level, idx, mine, theirs, *refs):
    later = lax.rem(idx[0] // (1 << level), 2) == 1
    last = level == 2
    if level:
        before, past, ahead, refs = refs[0], refs[1], refs[2], refs[3:]
    entering, decays = refs[0], refs[1]
    for k in range(8):
        m, t = mine[k].astype(F32), theirs[k].astype(F32)
        tm, tt = m[HD : HD + 1] + m[HD + 8 : HD + 9], t[HD : HD + 1] + t[HD + 8 : HD + 9]
        m, t = m[0:HD], t[0:HD]
        tp = past[k : k + 1, :] if level else jnp.ones((1, N), F32)
        ts = ahead[k : k + 1, :] if level else jnp.ones((1, N), F32)
        new = jnp.where(later, tp, 0.0) * t
        entering[k] = before[k] + new if level else new
        decays[0, k : k + 1, :] = tm
        decays[1, k : k + 1, :] = tt
        decays[2, k : k + 1, :] = ts
        if not last:
            total, past_out, ahead_out = refs[2:]
            past_out[k : k + 1, :] = tp * jnp.where(later, tt, 1.0)
            ahead_out[k : k + 1, :] = ts * jnp.where(later, 1.0, tt)
            total[k, 0:HD, :] = jnp.where(later, tm * t + m, tt * m + t).astype(BF16)
            tail = jnp.broadcast_to(tm * tt, (8, N))
            hi = tail.astype(BF16).astype(F32)
            total[k, HD:, :] = jnp.concatenate([hi, tail - hi], axis=0).astype(BF16)


def chip_adjoint(idx, mine, theirs, pay_mine, pay_theirs, out):
    c = idx[1]
    for k in range(8):
        h = c * 8 + k
        m, t = mine[h].astype(F32), theirs[h].astype(F32)
        ta = jnp.where(c == 0, decay_of(pay_mine[h]), decay_of(pay_theirs[h]))
        a = jnp.where(c == 0, m, t)
        b = jnp.where(c == 0, t, m)
        out[k] = (a + ta * b).astype(BF16)


def merge_adjoint(level, idx, decays, mine, theirs, *refs):
    later = lax.rem(idx[0] // (1 << level), 2) == 1
    if level:
        before, refs = refs[0], refs[1:]
    for k in range(8):
        m, t = mine[k].astype(F32), theirs[k].astype(F32)
        tm, tt, ts = (decays[i, k : k + 1, :] for i in range(3))
        new = jnp.where(later, 0.0, ts) * t
        refs[0][k] = before[k] + new if level else new
        if level < 2:
            refs[1][k] = jnp.where(later, t + tt * m, m + tm * t).astype(BF16)


def place_states(idx, mine, theirs, local, pay, out, needs):
    c = idx[1]
    for k in range(8):
        for group, ref in ((c * 8, mine), (8 - c * 8, theirs)):
            h = group + k
            e = ref[k]
            past = decay_of(pay[h]) * e + local[h, 0:HD, :].astype(F32)
            at = pl.multiple_of(h * HD, HD)
            out[pl.ds(at, HD), :] = jnp.where(c == needs, past, e).astype(BF16)


def causal(vecs, vecst, transposed):
    row = lax.broadcasted_iota(jnp.int32, (T, T), 0)
    col = lax.broadcasted_iota(jnp.int32, (T, T), 1)
    order = row <= col if transposed else row >= col
    same = vecst[:, SEG : SEG + 1] == vecs[SEG : SEG + 1, :]
    return jnp.where(jnp.logical_and(order, same), 0.0, -1e30)


def inner_part(vecs, vecst, x, b, c, out):
    scores = nt(c[...], b[...])
    mask = causal(vecs, vecst, False)
    for j in range(H // 2):
        xs = halves(x[:, j * 128 : (j + 1) * 128])
        acc = None
        for k in range(2):
            h = 2 * j + k
            decay = jnp.exp2(
                vecst[:, CUM + h : CUM + h + 1] - vecs[CUMDT + h : CUMDT + h + 1, :] + mask
            )
            term = nn((decay * scores).astype(BF16), xs[k])
            acc = term if acc is None else acc + term
        out[:, j * 128 : (j + 1) * 128] = acc


def forward_out(idx, skip, vecst, x, c, inner, mine, theirs, pay, yy, rounded, state):
    place_states(idx, mine, theirs, pay, pay, state, 1)
    for j in range(H // 2):
        cols = slice(j * 128, (j + 1) * 128)
        carried = nt(c[...], state[j * 128 : (j + 1) * 128, :])
        y = inner[:, cols] + carried * pair_columns(vecst, REACH, j)
        yy[:, cols] = y
        rounded[:, cols] = (y + pair_scalars(skip, j) * x[:, cols].astype(F32)).astype(BF16)


def weight_part(idx, cot, cot_t, mine, theirs, *refs):
    y = idx[3]
    outs, buf = refs[:5], refs[5]
    p0, p1, p2a, p2b, p3 = outs
    for n in range(4):
        cols = slice(n * 256, (n + 1) * 256)
        r = tn(cot[...], mine[:, cols]) + tn(cot_t[...], theirs[:, cols])
        buf[:, :, :, cols] = r.reshape(Z, Y, 32, 256).astype(BF16)
    p0[...] = buf[:, y]
    p1[...] = buf[:, (y + 1) % Y]
    p2a[...] = buf[:, (y + 2) % Y, :, 0:512]
    p2b[...] = buf[:, (y + 2) % Y, :, 512:]
    p3[...] = buf[:, (y + 3) % Y]


def relay_rows(p1, p3, via_a, via_b, q1, q3):
    q1[:, :, 0:512] = (p1[:, :, 0:512].astype(F32) + via_a[...].astype(F32)).astype(BF16)
    q1[:, :, 512:] = p1[:, :, 512:]
    q3[:, :, 0:512] = p3[:, :, 0:512]
    q3[:, :, 512:] = (p3[:, :, 512:].astype(F32) + via_b[...].astype(F32)).astype(BF16)


def sum_rows(idx, p0, left, right, keep, send):
    bit = lax.rem(idx[0], 2)
    for j in range(4):
        for out, b in ((keep, bit), (send, 1 - bit)):
            k = 2 * j + b
            s = p0[k].astype(F32) + left[k].astype(F32) + right[k].astype(F32)
            out[j] = s.astype(out.dtype)


def spread_rows(idx, mine, theirs, own, one, two, three):
    j = idx[0] // 2
    own[...] = mine[j] + theirs[j].astype(F32)
    for k, out in enumerate((one, two, three)):
        i = (j + k + 1) % 4
        out[...] = (mine[i] + theirs[i].astype(F32)).astype(BF16)


def last_rows(own, one, two, three, out):
    s = own[...] + one[...].astype(F32) + two[...].astype(F32) + three[...].astype(F32)
    out[...] = s * (1.0 / 128.0)


def out_grad(idx, cot, cot_t, here, left, right, far_a, far_b, own, send, weights):
    z, y = idx[0], idx[3]
    for d in range(Z):
        at = (z - d + Z) % Z
        weights[at, y] = here[d]
        weights[at, (y + 3) % Y] = left[d]
        weights[at, (y + 1) % Y] = right[d]
        weights[at, (y + 2) % Y] = far_a[d] if d < 4 else far_b[d - 4]
    for n in range(4):
        cols = slice(n * 256, (n + 1) * 256)
        w = weights[:, :, :, cols].reshape(FC, 256)
        send[:, cols] = nn(cot_t[...], w).astype(BF16)
        own[:, cols] = nn(cot[...], w)


def local_adjoint(vecst, own, got, c, g, adj):
    for j in range(H // 2):
        cols = slice(j * 128, (j + 1) * 128)
        gj = (own[:, cols] + got[:, cols].astype(F32)).astype(BF16)
        g[:, cols] = gj
        gr = (gj.astype(F32) * pair_columns(vecst, REACH, j)).astype(BF16)
        s = tn(gr, c[...])
        adj[2 * j] = s[0:HD].astype(BF16)
        adj[2 * j + 1] = s[HD:].astype(BF16)


def inner_grads(vecs, vecst, x, b, c, g, state, dx, dc, db):
    scores = nt(b[...], c[...])
    mask = causal(vecs, vecst, True)
    dscores = jnp.zeros((T, T), F32)
    dstate = jnp.zeros((T, N), F32)
    for j in range(H // 2):
        cols = slice(j * 128, (j + 1) * 128)
        gj = g[:, cols]
        gs, xs = halves(gj), halves(x[:, cols])
        acc = None
        for k in range(2):
            h = 2 * j + k
            decay = jnp.exp2(
                vecs[CUM + h : CUM + h + 1, :] - vecst[:, CUMDT + h : CUMDT + h + 1] + mask
            )
            term = nn((decay * scores).astype(BF16), gs[k])
            acc = term if acc is None else acc + term
            dscores = dscores + nt(xs[k], gj) * decay
        dx[:, cols] = acc
        gr = (gj.astype(F32) * pair_columns(vecst, REACH, j)).astype(BF16)
        dstate = dstate + nn(gr, state[j * 128 : (j + 1) * 128, :])
    ds = dscores.astype(BF16)
    db[...] = nn(ds, c[...])
    dc[...] = tn(ds, b[...]) + dstate


def two_part(ones, v):
    hi = v.astype(BF16)
    lo = (v - hi.astype(F32)).astype(BF16)
    return nt(ones, hi) + nt(ones, lo)


def final_grads(
    idx, skip, dlog, vecs, vecst, x, b, g, yy, dxm, dbp, state, mine, theirs, adjt, pay,
    dc, dx, maps, dstep, adj, flow, direct,
):
    place_states(idx, mine, theirs, adjt, pay, adj, 0)
    dbs = dbp[...]
    ends = []
    for j in range(H // 2):
        cols = slice(j * 128, (j + 1) * 128)
        rows = slice(j * 128, (j + 1) * 128)
        end = pair_columns(vecst, END, j)
        xj = x[:, cols].astype(F32)
        gj = g[:, cols].astype(F32)
        dxe = end * nt(b[...], adj[rows, :])
        dxx = dxm[:, cols] + dxe
        dx[:, cols] = (dxx + pair_scalars(skip, j) * gj).astype(BF16)
        dbs = dbs + nn((xj * end).astype(BF16), adj[rows, :])
        prod = xj * dxx
        direct[:, cols] = prod
        flow[:, cols] = gj * yy[:, cols] - prod
        ends.append(jnp.sum(xj * dxe, axis=0, keepdims=True))
    maps[:, 0:N] = dbs.astype(BF16)
    maps[:, N:] = dc[...].astype(BF16)
    head = lax.broadcasted_iota(jnp.int32, (H, W), 0)
    lane = lax.broadcasted_iota(jnp.int32, (H, W), 1)
    member = jnp.logical_and(lane >= head * HD, lane < head * HD + HD)
    ones = member.astype(BF16)
    dcum = two_part(ones, flow[...])
    ddt = two_part(ones, direct[...])
    total = jnp.sum(jnp.where(member, jnp.concatenate(ends, axis=1), 0.0), axis=1, keepdims=True)
    cross = jnp.sum(adj[...].astype(F32) * state[...].astype(F32), axis=1, keepdims=True)
    hi = cross.astype(BF16).astype(F32)
    cross = nn(ones, jnp.broadcast_to(hi, (W, 128)).astype(BF16)) + nn(
        ones, jnp.broadcast_to(cross - hi, (W, 128)).astype(BF16)
    )
    row = lax.broadcasted_iota(jnp.int32, (T, T), 0)
    col = lax.broadcasted_iota(jnp.int32, (T, T), 1)
    da = nn(dcum, (row >= col).astype(F32), precision=HIGH)
    da = da + total + vecs[THRU : THRU + H, 0:1] * cross[:, 0:1]
    ddt = ddt / vecs[DT : DT + H, :] - jnp.exp(head_column(dlog)) * da
    dstep[...] = ddt * vecs[SIG : SIG + H, :]


def sum_maps(*refs):
    s = sum(r[...].astype(F32) for r in refs[:-2]).astype(BF16)
    refs[-2][...] = s[:, 0:N]
    refs[-1][...] = s[:, N:]


def shift(v, axis, count, d):
    return lax.ppermute(v, axis, [(i, (i + d) % count) for i in range(count)])


def swap(v):
    return lax.ppermute(v, "core", [(0, 1), (1, 0)])


def facing(v, level):
    if level == 2:
        return lax.ppermute(v, "z", [(i, Z - 1 - i) for i in range(Z)])
    return lax.ppermute(v, "z", [(i, i ^ (1 << level)) for i in range(Z)])


def after(v, *others):
    return lax.optimization_barrier((v, others))[0]


def far_halves(left, right, axis, count):
    half = left.shape[0] // 2
    return shift(left[:half], axis, count, 1), shift(right[half:], axis, count, -1)


def on_device(
    ssm_input, input_map, output_map, step_raw, step_bias, decay_log, skip_gain, doc_lengths,
    out_weight, cotangent,
):
    x, b, c = ssm_input[0], input_map[0], output_map[0]
    raw = step_raw[0]
    idx = jnp.stack([lax.axis_index(a) for a in ("z", "core", "head", "fsdp")]).astype(jnp.int32)

    steps = [out_weight] + [None] * 7
    steps[1], steps[7] = shift(out_weight, "z", Z, 1), shift(out_weight, "z", Z, -1)

    pay, vecs, vecst = call(
        local_state,
        [((H, PAY, N), BF16), ((128, T), F32), ((T, 128), F32)],
        [idx, doc_lengths, step_bias, decay_log, raw, x, b],
        smem=(0, 1, 2, 3),
        hbm=(4, 5, 6),
        scratch=[
            pltpu.VMEM((H, T), F32),
            pltpu.VMEM((T, W), BF16),
            pltpu.VMEM((T, N), BF16),
            pltpu.SemaphoreType.DMA((3,)),
        ],
    )
    pay_t = swap(pay)
    steps[2] = shift(after(out_weight, pay), "z", Z, 2)
    (block,) = call(chip_state, [((8, PAY, N), BF16)], [idx, pay, pay_t], smem=(0,))

    def join_states(level, block, got, carry):
        outs = [((8, HD, N), F32), ((3, 8, N), F32)]
        if level < 2:
            outs += [((8, PAY, N), BF16), ((8, N), F32), ((8, N), F32)]
        mine, decay, *rest = call(
            functools.partial(merge_state, level), outs, [idx, block, got, *carry], smem=(0,)
        )
        return mine, decay, rest

    got = facing(block, 0)
    held, cot_here = after((out_weight, cotangent[0]), block)
    steps[6], steps[3] = shift(held, "z", Z, 6), shift(held, "z", Z, 3)
    mine, decay0, rest = join_states(0, block, got, [])
    block, carry = rest[0], [mine, *rest[1:]]
    got = facing(block, 1)
    held = after(out_weight, block)
    steps[5], steps[4] = shift(held, "z", Z, 5), shift(held, "z", Z, 4)
    cot_left, cot_right = shift(cot_here, "head", X, 1), shift(cot_here, "head", X, -1)
    cot_far = shift(after(cot_here, block), "head", X, 2)
    (bundle,) = call(stack_rows, [((Z, 32, W), BF16)], steps)
    w_left, w_right = shift(bundle, "fsdp", Y, 1), shift(bundle, "fsdp", Y, -1)
    mine, decay1, rest = join_states(1, block, got, carry)
    block, carry = rest[0], [mine, *rest[1:]]
    got = facing(block, 2)
    w_far = far_halves(w_left, w_right, "fsdp", Y)
    bundles = [bundle, w_left, w_right, *w_far]
    cot, cot_send = call(
        join_cot,
        [((T, FC), BF16)] * 2,
        [idx, cot_here, cot_left, cot_right, cot_far],
        smem=(0,),
    )
    cot_t = swap(cot_send)
    (inner,) = call(inner_part, [((T, W), F32)], [vecs, vecst, x, b, c])
    mine, decay2, _ = join_states(2, block, got, carry)
    decays = [decay0, decay1, decay2]
    theirs = swap(mine)
    yy, rounded, state = call(
        forward_out,
        [((T, W), F32), ((T, W), BF16), ((W, N), BF16)],
        [idx, skip_gain, vecst, x, c, inner, mine, theirs, pay_t],
        smem=(0, 1),
    )

    rounded_t = swap(rounded)
    p0, p1, p2a, p2b, p3 = call(
        weight_part,
        [((Z, 32, W), BF16)] * 2 + [((Z, 32, W // 2), BF16)] * 2 + [((Z, 32, W), BF16)],
        [idx, cot, cot_t, rounded, rounded_t],
        smem=(0,),
        scratch=[pltpu.VMEM((Z, Y, 32, W), BF16)],
    )
    via_a, via_b = shift(p2a, "fsdp", Y, 1), shift(p2b, "fsdp", Y, -1)

    part, part_t = call(
        out_grad,
        [((T, W), F32), ((T, W), BF16)],
        [idx, cot, cot_t, *bundles],
        smem=(0,),
        scratch=[pltpu.VMEM((Z, Y, 32, W), BF16)],
    )
    g, adj = call(
        local_adjoint, [((T, W), BF16), ((H, HD, N), BF16)], [vecst, part, swap(part_t), c]
    )
    adj_t = swap(adj)
    (block,) = call(
        chip_adjoint, [((8, HD, N), BF16)], [idx, adj, adj_t, pay, pay_t], smem=(0,)
    )
    got = facing(block, 0)
    via_a, via_b = after((via_a, via_b), block)
    q1, q3 = call(
        relay_rows,
        [((Z, 32, W), BF16)] * 2,
        [p1, p3, via_a, via_b],
    )
    keep, send = call(
        sum_rows,
        [((4, 32, W), F32), ((4, 32, W), BF16)],
        [idx, p0, shift(q1, "fsdp", Y, 1), shift(q3, "fsdp", Y, -1)],
        smem=(0,),
    )
    paired = lax.ppermute(send, "z", [(i, i ^ 1) for i in range(Z)])
    own, *parts = call(
        spread_rows,
        [((32, W), F32)] + [((32, W), BF16)] * 3,
        [idx, keep, paired],
        smem=(0,),
    )
    parts = [shift(v, "z", Z, 2 * k + 2) for k, v in enumerate(parts)]
    (weight_grad,) = call(last_rows, [((32, W), F32)], [own, *parts])

    dxm, dc, dbp = call(
        inner_grads,
        [((T, W), F32), ((T, N), F32), ((T, N), F32)],
        [vecs, vecst, x, b, c, g, state],
    )
    carry = []
    for level in range(3):
        outs = [((8, HD, N), F32)] + [((8, HD, N), BF16)] * (level < 2)
        mine, *rest = call(
            functools.partial(merge_adjoint, level),
            outs,
            [idx, decays[level], block, got, *carry],
            smem=(0,),
        )
        if rest:
            block, carry = rest[0], [mine]
            got = facing(block, level + 1)
            got = after(got, dxm)
    theirs = swap(mine)
    dx, maps, dstep = call(
        final_grads,
        [((T, W), BF16), ((T, 2 * N), BF16), ((H, T), F32)],
        [idx, skip_gain, decay_log, vecs, vecst, x, b, g, yy, dxm, dbp, state, mine, theirs, adj_t, pay_t, dc],
        smem=(0, 1, 2),
        scratch=[pltpu.VMEM((W, N), BF16), pltpu.VMEM((T, W), F32), pltpu.VMEM((T, W), F32)],
    )
    db, dc = call(
        sum_maps,
        [((T, N), BF16)] * 2,
        [maps] + [shift(maps, "head", X, d) for d in (1, 2, 3)],
    )
    return dx[None], db[None], dc[None], dstep[None], weight_grad


def solution(mesh):
    inner = Mesh(mesh.devices.reshape(Z, 2, X, Y), ("z", "core", "head", "fsdp"))
    ctx = ("z", "core")
    features = ("z", "core", "fsdp")
    return jax.shard_map(
        on_device,
        mesh=inner,
        in_specs=(
            P("fsdp", ctx, "head"),
            P("fsdp", ctx, None),
            P("fsdp", ctx, None),
            P("fsdp", "head", ctx),
            P("head"),
            P("head"),
            P("head"),
            P("fsdp", None),
            P(features, "head"),
            P("fsdp", ctx, "head"),
        ),
        out_specs=(
            P("fsdp", ctx, "head"),
            P("fsdp", ctx, None),
            P("fsdp", ctx, None),
            P("fsdp", "head", ctx),
            P(features, "head"),
        ),
        check_vma=False,
    )
```

```python
import functools
import math

import jax
import jax.numpy as jnp
from jax import lax
from jax.experimental import pallas as pl
from jax.experimental.pallas import tpu as pltpu
from jax.sharding import Mesh, PartitionSpec as P

F32 = jnp.float32
BF16 = jnp.bfloat16
LOG2E = 1.4426950408889634
HIGH = lax.Precision.HIGHEST

T = 256
H = 16
HD = 64
N = 128
W = H * HD
FC = 1024
Z, Y, X = 8, 4, 4
STEPS = (0, 1, 7, 2, 6), (3, 5, 4)
PAY = HD + 16

WEIGHT = {
    "merge_state1": 8,
    "out_grad": 1,
    "weight_part": 0.1,
    "inner_grads": 0.6,
    "final_maps": 2,
    "forward_out": 2,
    "merge_state0": 2,
}

CUM, CUMDT, REACH, END, DT, SIG, THRU, SEG = range(0, 128, 16)


def nt(a, b, **kw):
    return lax.dot_general(a, b, (((1,), (1,)), ((), ())), preferred_element_type=F32, **kw)


def nn(a, b, **kw):
    return lax.dot_general(a, b, (((1,), (0,)), ((), ())), preferred_element_type=F32, **kw)


def tn(a, b, **kw):
    return lax.dot_general(a, b, (((0,), (0,)), ((), ())), preferred_element_type=F32, **kw)


def label_of(body):
    if hasattr(body, "func"):
        return body.func.__name__ + (str(body.args[0]) if isinstance(body.args[0], int) else "")
    return body.__name__


def call(body, outs, ins, smem=(), hbm=(), scratch=(), limit=40):
    shapes = [jax.ShapeDtypeStruct(s, d) for s, d in outs]
    specs = [
        pl.BlockSpec(
            memory_space=pltpu.SMEM if i in smem else pltpu.HBM if i in hbm else pltpu.VMEM
        )
        for i in range(len(ins))
    ]
    return pl.pallas_call(
        body,
        out_shape=shapes,
        in_specs=specs,
        out_specs=[pl.BlockSpec(memory_space=pltpu.VMEM)] * len(shapes),
        scratch_shapes=list(scratch),
        compiler_params=pltpu.CompilerParams(vmem_limit_bytes=limit << 20),
        cost_estimate=pl.CostEstimate(
            flops=int(WEIGHT.get(label_of(body), 0) * 1.15e9) + 1,
            bytes_accessed=1,
            transcendentals=0,
        ),
    )(*ins)


def pair_columns(vt_ref, group, j):
    low = lax.broadcasted_iota(jnp.int32, (T, 128), 1) < HD
    a = vt_ref[:, group + 2 * j : group + 2 * j + 1]
    b = vt_ref[:, group + 2 * j + 1 : group + 2 * j + 2]
    return jnp.where(low, a, b)


def pair_scalars(ref, j):
    low = lax.broadcasted_iota(jnp.int32, (1, 128), 1) < HD
    return jnp.where(low, ref[2 * j], ref[2 * j + 1])


def halves(v):
    low = (lax.broadcasted_iota(jnp.int32, (1, 128), 1) < HD).astype(v.dtype)
    return v * low, v * (1 - low)


def stack_rows(*refs):
    for i, ref in enumerate(refs[:-1]):
        refs[-1][i] = ref[...]


def join_cot(idx, here, left, right, far_a, far_b, own, send):
    c, x = idx[1], idx[2]
    half = T // 2
    for d, parts in (
        (0, ((here, 0, T),)),
        (1, ((left, 0, T),)),
        (2, ((far_a, 0, half), (far_b, half, half))),
        (3, ((right, 0, T),)),
    ):
        base = ((x - d + X) % X) * 256
        for k in range(2):
            to = pl.ds(pl.multiple_of(base + k * 128, 128), 128)
            at = pl.ds(pl.multiple_of(k * 256 + c * 128, 128), 128)
            other = pl.ds(pl.multiple_of(k * 256 + (1 - c) * 128, 128), 128)
            for ref, start, size in parts:
                own[start : start + size, to] = ref[:, at]
                send[start : start + size, to] = ref[:, other]


def head_column(ref):
    head = lax.broadcasted_iota(jnp.int32, (H, 1), 0)
    out = jnp.zeros((H, 1), F32)
    for h in range(H):
        out = jnp.where(head == h, ref[h], out)
    return out


def local_state(
    idx, lens, bias, dlog, raw_hbm, x_hbm, b_hbm, pay, vecs, vecst, raw, x, b, sems
):
    copies = [
        pltpu.make_async_copy(src, dst, sems.at[i])
        for i, (src, dst) in enumerate(((raw_hbm, raw), (x_hbm, x), (b_hbm, b)))
    ]
    for copy in copies:
        copy.start()
    base = (idx[0] * 2 + idx[1]) * T
    copies[0].wait()
    v = raw[...] + head_column(bias)
    dt = jnp.maximum(v, 0.0) + jnp.log1p(jnp.exp(-jnp.abs(v)))
    a = -jnp.exp(head_column(dlog)) * dt * LOG2E
    row = lax.broadcasted_iota(jnp.int32, (T, T), 0)
    col = lax.broadcasted_iota(jnp.int32, (T, T), 1)
    cum = nn(a, (row <= col).astype(F32), precision=HIGH)
    cumdt = cum - jnp.log(dt) * LOG2E
    pos = base + lax.broadcasted_iota(jnp.int32, (H, T), 1)
    seg = jnp.zeros((H, T), F32)
    last = jnp.float32(0)
    first = jnp.int32(0)
    for k in range(8):
        here = first >= base
        seg = seg + jnp.where(jnp.logical_and(here, pos >= first), 1.0, 0.0)
        last = last + jnp.where(jnp.logical_and(here, first < base + T), 1.0, 0.0)
        first = first + lens[0, k]
    end = jnp.where(seg == last, jnp.exp2(cum[:, T - 1 :] - cumdt), 0.0)
    reach = jnp.where(seg == 0.0, jnp.exp2(cum), 0.0)
    thru = jnp.where(last == 0.0, jnp.exp2(cum[:, T - 1 :]), 0.0)
    thru = jnp.broadcast_to(thru, (H, T))
    for at, value in (
        (CUM, cum),
        (CUMDT, cumdt),
        (REACH, reach),
        (END, end),
        (DT, dt),
        (SIG, jax.nn.sigmoid(v)),
        (THRU, thru),
        (SEG, seg),
    ):
        vecs[at : at + H, :] = value
    vecst[...] = vecs[...].T
    copies[1].wait()
    copies[2].wait()
    for j in range(H // 2):
        xs = x[:, j * 128 : (j + 1) * 128].astype(F32) * pair_columns(vecst, END, j)
        s = tn(xs.astype(BF16), b[...])
        pay[2 * j, 0:HD, :] = s[0:HD].astype(BF16)
        pay[2 * j + 1, 0:HD, :] = s[HD:].astype(BF16)
    hi = thru.astype(BF16)
    lo = (thru - hi.astype(F32)).astype(BF16)
    for h in range(H):
        pay[h, HD : HD + 8, :] = jnp.broadcast_to(hi[h : h + 1, 0:128].astype(F32), (8, 128)).astype(BF16)
        pay[h, HD + 8 :, :] = jnp.broadcast_to(lo[h : h + 1, 0:128].astype(F32), (8, 128)).astype(BF16)


def decay_of(block):
    tail = block[HD:, :].astype(F32)
    return tail[0:1] + tail[8:9]


def chip_state(idx, mine, theirs, out):
    c = idx[1]
    for k in range(8):
        m, t = mine[c * 8 + k], theirs[c * 8 + k]
        a = jnp.where(c == 0, m.astype(F32), t.astype(F32))
        b = jnp.where(c == 0, t.astype(F32), m.astype(F32))
        ta = a[HD : HD + 1] + a[HD + 8 : HD + 9]
        tb = b[HD : HD + 1] + b[HD + 8 : HD + 9]
        out[k, 0:HD, :] = (tb * a[0:HD] + b[0:HD]).astype(BF16)
        t = jnp.broadcast_to(ta * tb, (8, 128))
        hi = t.astype(BF16).astype(F32)
        out[k, HD:, :] = jnp.concatenate([hi, t - hi], axis=0).astype(BF16)


def merge_state(level, idx, mine, theirs, *refs):
    later = lax.rem(idx[0] // (1 << level), 2) == 1
    last = level == 2
    if level:
        before, past, ahead, refs = refs[0], refs[1], refs[2], refs[3:]
    entering, decays = refs[0], refs[1]
    for k in range(8):
        m, t = mine[k].astype(F32), theirs[k].astype(F32)
        tm, tt = m[HD : HD + 1] + m[HD + 8 : HD + 9], t[HD : HD + 1] + t[HD + 8 : HD + 9]
        m, t = m[0:HD], t[0:HD]
        tp = past[k : k + 1, :] if level else jnp.ones((1, N), F32)
        ts = ahead[k : k + 1, :] if level else jnp.ones((1, N), F32)
        new = jnp.where(later, tp, 0.0) * t
        entering[k] = before[k] + new if level else new
        decays[0, k : k + 1, :] = tm
        decays[1, k : k + 1, :] = tt
        decays[2, k : k + 1, :] = ts
        if not last:
            total, past_out, ahead_out = refs[2:]
            past_out[k : k + 1, :] = tp * jnp.where(later, tt, 1.0)
            ahead_out[k : k + 1, :] = ts * jnp.where(later, 1.0, tt)
            total[k, 0:HD, :] = jnp.where(later, tm * t + m, tt * m + t).astype(BF16)
            tail = jnp.broadcast_to(tm * tt, (8, N))
            hi = tail.astype(BF16).astype(F32)
            total[k, HD:, :] = jnp.concatenate([hi, tail - hi], axis=0).astype(BF16)


def chip_adjoint(idx, mine, theirs, pay_mine, pay_theirs, out):
    c = idx[1]
    for k in range(8):
        h = c * 8 + k
        m, t = mine[h].astype(F32), theirs[h].astype(F32)
        ta = jnp.where(c == 0, decay_of(pay_mine[h]), decay_of(pay_theirs[h]))
        a = jnp.where(c == 0, m, t)
        b = jnp.where(c == 0, t, m)
        out[k] = (a + ta * b).astype(BF16)


def merge_adjoint(level, idx, decays, mine, theirs, *refs):
    later = lax.rem(idx[0] // (1 << level), 2) == 1
    if level:
        before, refs = refs[0], refs[1:]
    for k in range(8):
        m, t = mine[k].astype(F32), theirs[k].astype(F32)
        tm, tt, ts = (decays[i, k : k + 1, :] for i in range(3))
        new = jnp.where(later, 0.0, ts) * t
        refs[0][k] = before[k] + new if level else new
        if level < 2:
            refs[1][k] = jnp.where(later, t + tt * m, m + tm * t).astype(BF16)


def place_states(idx, mine, theirs, local, pay, out, needs):
    c = idx[1]
    for k in range(8):
        for group, ref in ((c * 8, mine), (8 - c * 8, theirs)):
            h = group + k
            e = ref[k]
            past = decay_of(pay[h]) * e + local[h, 0:HD, :].astype(F32)
            at = pl.multiple_of(h * HD, HD)
            out[pl.ds(at, HD), :] = jnp.where(c == needs, past, e).astype(BF16)


def causal(vecs, vecst, transposed):
    row = lax.broadcasted_iota(jnp.int32, (T, T), 0)
    col = lax.broadcasted_iota(jnp.int32, (T, T), 1)
    order = row <= col if transposed else row >= col
    same = vecst[:, SEG : SEG + 1] == vecs[SEG : SEG + 1, :]
    return jnp.where(jnp.logical_and(order, same), 0.0, -1e30)


def inner_part(vecs, vecst, x, b, c, out):
    scores = nt(c[...], b[...])
    mask = causal(vecs, vecst, False)
    for j in range(H // 2):
        xs = halves(x[:, j * 128 : (j + 1) * 128])
        acc = None
        for k in range(2):
            h = 2 * j + k
            decay = jnp.exp2(
                vecst[:, CUM + h : CUM + h + 1] - vecs[CUMDT + h : CUMDT + h + 1, :] + mask
            )
            term = nn((decay * scores).astype(BF16), xs[k])
            acc = term if acc is None else acc + term
        out[:, j * 128 : (j + 1) * 128] = acc


def forward_out(idx, skip, vecst, x, c, inner, mine, theirs, pay, yy, rounded, state):
    place_states(idx, mine, theirs, pay, pay, state, 1)
    for j in range(H // 2):
        cols = slice(j * 128, (j + 1) * 128)
        carried = nt(c[...], state[j * 128 : (j + 1) * 128, :])
        y = inner[:, cols] + carried * pair_columns(vecst, REACH, j)
        yy[:, cols] = y
        rounded[:, cols] = (y + pair_scalars(skip, j) * x[:, cols].astype(F32)).astype(BF16)


def weight_part(idx, cot, cot_t, mine, theirs, *refs):
    y = idx[3]
    outs, buf = refs[:5], refs[5]
    p0, p1, p2a, p2b, p3 = outs
    for n in range(4):
        cols = slice(n * 256, (n + 1) * 256)
        r = tn(cot[...], mine[:, cols]) + tn(cot_t[...], theirs[:, cols])
        buf[:, :, :, cols] = r.reshape(Z, Y, 32, 256).astype(BF16)
    p0[...] = buf[:, y]
    p1[...] = buf[:, (y + 1) % Y]
    p2a[...] = buf[:, (y + 2) % Y, :, 0:512]
    p2b[...] = buf[:, (y + 2) % Y, :, 512:]
    p3[...] = buf[:, (y + 3) % Y]


def relay_rows(p1, p3, via_a, via_b, q1, q3):
    q1[:, :, 0:512] = (p1[:, :, 0:512].astype(F32) + via_a[...].astype(F32)).astype(BF16)
    q1[:, :, 512:] = p1[:, :, 512:]
    q3[:, :, 0:512] = p3[:, :, 0:512]
    q3[:, :, 512:] = (p3[:, :, 512:].astype(F32) + via_b[...].astype(F32)).astype(BF16)


def sum_rows(idx, p0, left, right, keep, send):
    bit = lax.rem(idx[0], 2)
    for j in range(4):
        for out, b in ((keep, bit), (send, 1 - bit)):
            k = 2 * j + b
            s = p0[k].astype(F32) + left[k].astype(F32) + right[k].astype(F32)
            out[j] = s.astype(out.dtype)


def spread_rows(idx, mine, theirs, own, one, two, three):
    j = idx[0] // 2
    own[...] = mine[j] + theirs[j].astype(F32)
    for k, out in enumerate((one, two, three)):
        i = (j + k + 1) % 4
        out[...] = (mine[i] + theirs[i].astype(F32)).astype(BF16)


def last_rows(own, one, two, three, out):
    s = own[...] + one[...].astype(F32) + two[...].astype(F32) + three[...].astype(F32)
    out[...] = s * (1.0 / 128.0)


def out_grad(idx, cot, cot_t, *refs):
    z, y = idx[0], idx[3]
    bundles, own, send, weights = refs[:8], refs[8], refs[9], refs[10]
    for i, d in enumerate((0, -1, 1, 2)):
        for group, steps in enumerate(STEPS):
            for k, step in enumerate(steps):
                weights[(z - step + Z) % Z, (y + d + Y) % Y] = bundles[2 * i + group][k]
    for n in range(4):
        cols = slice(n * 256, (n + 1) * 256)
        w = weights[:, :, :, cols].reshape(FC, 256)
        send[:, cols] = nn(cot_t[...], w).astype(BF16)
        own[:, cols] = nn(cot[...], w)


def local_adjoint(vecst, own, got, c, g, adj):
    for j in range(H // 2):
        cols = slice(j * 128, (j + 1) * 128)
        gj = (own[:, cols] + got[:, cols].astype(F32)).astype(BF16)
        g[:, cols] = gj
        gr = (gj.astype(F32) * pair_columns(vecst, REACH, j)).astype(BF16)
        s = tn(gr, c[...])
        adj[2 * j] = s[0:HD].astype(BF16)
        adj[2 * j + 1] = s[HD:].astype(BF16)


def inner_grads(vecs, vecst, x, b, c, g, state, dx, dc, db):
    scores = nt(b[...], c[...])
    mask = causal(vecs, vecst, True)
    dscores = jnp.zeros((T, T), F32)
    dstate = jnp.zeros((T, N), F32)
    for j in range(H // 2):
        cols = slice(j * 128, (j + 1) * 128)
        gj = g[:, cols]
        gs, xs = halves(gj), halves(x[:, cols])
        acc = None
        for k in range(2):
            h = 2 * j + k
            decay = jnp.exp2(
                vecs[CUM + h : CUM + h + 1, :] - vecst[:, CUMDT + h : CUMDT + h + 1] + mask
            )
            term = nn((decay * scores).astype(BF16), gs[k])
            acc = term if acc is None else acc + term
            dscores = dscores + nt(xs[k], gj) * decay
        dx[:, cols] = acc
        gr = (gj.astype(F32) * pair_columns(vecst, REACH, j)).astype(BF16)
        dstate = dstate + nn(gr, state[j * 128 : (j + 1) * 128, :])
    ds = dscores.astype(BF16)
    db[...] = nn(ds, c[...])
    dc[...] = tn(ds, b[...]) + dstate


def two_part(ones, v):
    hi = v.astype(BF16)
    lo = (v - hi.astype(F32)).astype(BF16)
    return nt(ones, hi) + nt(ones, lo)


def final_maps(idx, vecst, x, dbp, dc, mine, theirs, adjt, pay, maps, adj):
    place_states(idx, mine, theirs, adjt, pay, adj, 0)
    dbs = dbp[...]
    for j in range(H // 2):
        cols = slice(j * 128, (j + 1) * 128)
        xe = x[:, cols].astype(F32) * pair_columns(vecst, END, j)
        dbs = dbs + nn(xe.astype(BF16), adj[cols, :])
    maps[:, 0:N] = dbs.astype(BF16)
    maps[:, N:] = dc[...].astype(BF16)


def final_grads(
    skip, dlog, vecs, vecst, x, b, g, yy, dxm, state, adj, dx, dstep, flow, direct
):
    ends = []
    for j in range(H // 2):
        cols = slice(j * 128, (j + 1) * 128)
        rows = slice(j * 128, (j + 1) * 128)
        end = pair_columns(vecst, END, j)
        xj = x[:, cols].astype(F32)
        gj = g[:, cols].astype(F32)
        dxe = end * nt(b[...], adj[rows, :])
        dxx = dxm[:, cols] + dxe
        dx[:, cols] = (dxx + pair_scalars(skip, j) * gj).astype(BF16)
        prod = xj * dxx
        direct[:, cols] = prod
        flow[:, cols] = gj * yy[:, cols] - prod
        ends.append(jnp.sum(xj * dxe, axis=0, keepdims=True))
    head = lax.broadcasted_iota(jnp.int32, (H, W), 0)
    lane = lax.broadcasted_iota(jnp.int32, (H, W), 1)
    member = jnp.logical_and(lane >= head * HD, lane < head * HD + HD)
    ones = member.astype(BF16)
    dcum = two_part(ones, flow[...])
    ddt = two_part(ones, direct[...])
    total = jnp.sum(jnp.where(member, jnp.concatenate(ends, axis=1), 0.0), axis=1, keepdims=True)
    cross = jnp.sum(adj[...].astype(F32) * state[...].astype(F32), axis=1, keepdims=True)
    hi = cross.astype(BF16).astype(F32)
    cross = nn(ones, jnp.broadcast_to(hi, (W, 128)).astype(BF16)) + nn(
        ones, jnp.broadcast_to(cross - hi, (W, 128)).astype(BF16)
    )
    row = lax.broadcasted_iota(jnp.int32, (T, T), 0)
    col = lax.broadcasted_iota(jnp.int32, (T, T), 1)
    da = nn(dcum, (row >= col).astype(F32), precision=HIGH)
    da = da + total + vecs[THRU : THRU + H, 0:1] * cross[:, 0:1]
    ddt = ddt / vecs[DT : DT + H, :] - jnp.exp(head_column(dlog)) * da
    dstep[...] = ddt * vecs[SIG : SIG + H, :]


def sum_maps(*refs):
    s = sum(r[...].astype(F32) for r in refs[:-2]).astype(BF16)
    refs[-2][...] = s[:, 0:N]
    refs[-1][...] = s[:, N:]


def shift(v, axis, count, d):
    return lax.ppermute(v, axis, [(i, (i + d) % count) for i in range(count)])


def swap(v):
    return lax.ppermute(v, "core", [(0, 1), (1, 0)])


def facing(v, level):
    if level == 2:
        return lax.ppermute(v, "z", [(i, Z - 1 - i) for i in range(Z)])
    return lax.ppermute(v, "z", [(i, i ^ (1 << level)) for i in range(Z)])


def after(v, *others):
    return lax.optimization_barrier((v, others))[0]


def far_halves(left, right, axis, count):
    half = left.shape[0] // 2
    return shift(left[:half], axis, count, 1), shift(right[half:], axis, count, -1)


def on_device(
    ssm_input, input_map, output_map, step_raw, step_bias, decay_log, skip_gain, doc_lengths,
    out_weight, cotangent,
):
    x, b, c = ssm_input[0], input_map[0], output_map[0]
    raw = step_raw[0]
    idx = jnp.stack([lax.axis_index(a) for a in ("z", "core", "head", "fsdp")]).astype(jnp.int32)

    r1, l1 = shift(out_weight, "z", Z, 1), shift(out_weight, "z", Z, -1)
    cot_here = cotangent[0]
    cot_left, cot_right = shift(cot_here, "head", X, 1), shift(cot_here, "head", X, -1)

    pay, vecs, vecst = call(
        local_state,
        [((H, PAY, N), BF16), ((128, T), F32), ((T, 128), F32)],
        [idx, doc_lengths, step_bias, decay_log, raw, x, b],
        smem=(0, 1, 2, 3),
        hbm=(4, 5, 6),
        scratch=[
            pltpu.VMEM((H, T), F32),
            pltpu.VMEM((T, W), BF16),
            pltpu.VMEM((T, N), BF16),
            pltpu.SemaphoreType.DMA((3,)),
        ],
    )
    pay, r1, l1 = lax.optimization_barrier((pay, r1, l1))
    pay_t = swap(pay)
    r2, l2 = shift(r1, "z", Z, 1), shift(l1, "z", Z, -1)
    (block,) = call(chip_state, [((8, PAY, N), BF16)], [idx, pay, pay_t], smem=(0,))

    def join_states(level, block, got, carry):
        outs = [((8, HD, N), F32), ((3, 8, N), F32)]
        if level < 2:
            outs += [((8, PAY, N), BF16), ((8, N), F32), ((8, N), F32)]
        mine, decay, *rest = call(
            functools.partial(merge_state, level), outs, [idx, block, got, *carry], smem=(0,)
        )
        return mine, decay, rest

    got = facing(block, 0)
    r2, l2 = after((r2, l2), block)
    r3, l3 = shift(r2, "z", Z, 1), shift(l2, "z", Z, -1)
    (near,) = call(stack_rows, [((5, 32, W), BF16)], [out_weight, r1, l1, r2, l2])
    near_left, near_right = shift(near, "fsdp", Y, 1), shift(near, "fsdp", Y, -1)
    cot_far = far_halves(*after((cot_left, cot_right), near), "head", X)
    mine, decay0, rest = join_states(0, block, got, [])
    block, carry = rest[0], [mine, *rest[1:]]
    got = facing(block, 1)
    r4 = shift(r3, "z", Z, 1)
    (rest_rows,) = call(stack_rows, [((3, 32, W), BF16)], [r3, l3, r4])
    rest_left, rest_right = shift(rest_rows, "fsdp", Y, 1), shift(rest_rows, "fsdp", Y, -1)
    near_far = shift(near_left, "fsdp", Y, 1)
    got, rest_rows = lax.optimization_barrier((got, rest_rows))
    mine, decay1, rest = join_states(1, block, got, carry)
    block, carry = rest[0], [mine, *rest[1:]]
    got = facing(block, 2)
    rest_far = shift(rest_right, "fsdp", Y, -1)
    bundles = [
        near, rest_rows, near_left, rest_left, near_right, rest_right, near_far, rest_far,
    ]
    cot, cot_send = call(
        join_cot,
        [((T, FC), BF16)] * 2,
        [idx, cot_here, cot_left, cot_right, *cot_far],
        smem=(0,),
    )
    cot_t = swap(cot_send)
    (inner,) = call(inner_part, [((T, W), F32)], [vecs, vecst, x, b, c])
    mine, decay2, _ = join_states(2, block, got, carry)
    decays = [decay0, decay1, decay2]
    theirs = swap(mine)
    yy, rounded, state = call(
        forward_out,
        [((T, W), F32), ((T, W), BF16), ((W, N), BF16)],
        [idx, skip_gain, vecst, x, c, inner, mine, theirs, pay_t],
        smem=(0, 1),
    )

    rounded_t = swap(rounded)
    p0, p1, p2a, p2b, p3 = call(
        weight_part,
        [((Z, 32, W), BF16)] * 2 + [((Z, 32, W // 2), BF16)] * 2 + [((Z, 32, W), BF16)],
        [idx, cot, cot_t, rounded, rounded_t],
        smem=(0,),
        scratch=[pltpu.VMEM((Z, Y, 32, W), BF16)],
    )
    via_a, via_b = shift(p2a, "fsdp", Y, 1), shift(p2b, "fsdp", Y, -1)

    part, part_t = call(
        out_grad,
        [((T, W), F32), ((T, W), BF16)],
        [idx, cot, cot_t, *bundles],
        smem=(0,),
        scratch=[pltpu.VMEM((Z, Y, 32, W), BF16)],
    )
    g, adj = call(
        local_adjoint, [((T, W), BF16), ((H, HD, N), BF16)], [vecst, part, swap(part_t), c]
    )
    adj_t = swap(adj)
    (block,) = call(
        chip_adjoint, [((8, HD, N), BF16)], [idx, adj, adj_t, pay, pay_t], smem=(0,)
    )
    got = facing(block, 0)
    via_a, via_b = after((via_a, via_b), block)
    q1, q3 = call(
        relay_rows,
        [((Z, 32, W), BF16)] * 2,
        [p1, p3, via_a, via_b],
    )
    keep, send = call(
        sum_rows,
        [((4, 32, W), F32), ((4, 32, W), BF16)],
        [idx, p0, shift(q1, "fsdp", Y, 1), shift(q3, "fsdp", Y, -1)],
        smem=(0,),
    )
    paired = lax.ppermute(send, "z", [(i, i ^ 1) for i in range(Z)])
    own, *parts = call(
        spread_rows,
        [((32, W), F32)] + [((32, W), BF16)] * 3,
        [idx, keep, paired],
        smem=(0,),
    )
    parts = [shift(v, "z", Z, 2 * k + 2) for k, v in enumerate(parts)]
    (weight_grad,) = call(last_rows, [((32, W), F32)], [own, *parts])

    dxm, dc, dbp = call(
        inner_grads,
        [((T, W), F32), ((T, N), F32), ((T, N), F32)],
        [vecs, vecst, x, b, c, g, state],
    )
    carry = []
    for level in range(3):
        outs = [((8, HD, N), F32)] + [((8, HD, N), BF16)] * (level < 2)
        mine, *rest = call(
            functools.partial(merge_adjoint, level),
            outs,
            [idx, decays[level], block, got, *carry],
            smem=(0,),
        )
        if rest:
            block, carry = rest[0], [mine]
            got = facing(block, level + 1)
            got = after(got, dxm)
    theirs = swap(mine)
    maps, adj = call(
        final_maps,
        [((T, 2 * N), BF16), ((W, N), BF16)],
        [idx, vecst, x, dbp, dc, mine, theirs, adj_t, pay_t],
        smem=(0,),
    )
    dx, dstep = call(
        final_grads,
        [((T, W), BF16), ((H, T), F32)],
        [skip_gain, decay_log, vecs, vecst, x, b, g, yy, dxm, state, adj],
        smem=(0, 1),
        scratch=[pltpu.VMEM((T, W), F32)] * 2,
    )
    db, dc = call(
        sum_maps,
        [((T, N), BF16)] * 2,
        [maps] + [shift(maps, "head", X, d) for d in (1, 2, 3)],
    )
    return dx[None], db[None], dc[None], dstep[None], weight_grad


def solution(mesh):
    inner = Mesh(mesh.devices.reshape(Z, 2, X, Y), ("z", "core", "head", "fsdp"))
    ctx = ("z", "core")
    features = ("z", "core", "fsdp")
    return jax.shard_map(
        on_device,
        mesh=inner,
        in_specs=(
            P("fsdp", ctx, "head"),
            P("fsdp", ctx, None),
            P("fsdp", ctx, None),
            P("fsdp", "head", ctx),
            P("head"),
            P("head"),
            P("head"),
            P("fsdp", None),
            P(features, "head"),
            P("fsdp", ctx, "head"),
        ),
        out_specs=(
            P("fsdp", ctx, "head"),
            P("fsdp", ctx, None),
            P("fsdp", ctx, None),
            P("fsdp", "head", ctx),
            P(features, "head"),
        ),
        check_vma=False,
    )
```

```python
import functools
import math

import jax
import jax.numpy as jnp
from jax import lax
from jax.experimental import pallas as pl
from jax.experimental.pallas import tpu as pltpu
from jax.sharding import Mesh, PartitionSpec as P

F32 = jnp.float32
BF16 = jnp.bfloat16
LOG2E = 1.4426950408889634
HIGH = lax.Precision.HIGHEST

T = 256
H = 16
HD = 64
N = 128
W = H * HD
FC = 1024
Z, Y, X = 8, 4, 4
STEPS = (0, 1, 7, 2, 6), (3, 5, 4)
PAY = HD + 16

WEIGHT = {
    "merge_state1": 8,
    "out_grad": 1,
    "weight_part": 0.1,
    "inner_grads": 0.6,
    "final_maps": 2,
    "forward_out": 2,
    "local_adjoint": 4,
    "merge_adjoint0": 0.1,
    "chip_state": 0.1,
    "merge_adjoint1": 2,
}

CUM, CUMDT, REACH, END, DT, SIG, THRU, SEG = range(0, 128, 16)


def nt(a, b, **kw):
    return lax.dot_general(a, b, (((1,), (1,)), ((), ())), preferred_element_type=F32, **kw)


def nn(a, b, **kw):
    return lax.dot_general(a, b, (((1,), (0,)), ((), ())), preferred_element_type=F32, **kw)


def tn(a, b, **kw):
    return lax.dot_general(a, b, (((0,), (0,)), ((), ())), preferred_element_type=F32, **kw)


def label_of(body):
    if hasattr(body, "func"):
        return body.func.__name__ + (str(body.args[0]) if isinstance(body.args[0], int) else "")
    return body.__name__


def call(body, outs, ins, smem=(), hbm=(), scratch=(), limit=40):
    shapes = [jax.ShapeDtypeStruct(s, d) for s, d in outs]
    specs = [
        pl.BlockSpec(
            memory_space=pltpu.SMEM if i in smem else pltpu.HBM if i in hbm else pltpu.VMEM
        )
        for i in range(len(ins))
    ]
    return pl.pallas_call(
        body,
        out_shape=shapes,
        in_specs=specs,
        out_specs=[pl.BlockSpec(memory_space=pltpu.VMEM)] * len(shapes),
        scratch_shapes=list(scratch),
        compiler_params=pltpu.CompilerParams(vmem_limit_bytes=limit << 20),
        cost_estimate=pl.CostEstimate(
            flops=int(WEIGHT.get(label_of(body), 0) * 1.15e9) + 1,
            bytes_accessed=1,
            transcendentals=0,
        ),
    )(*ins)


def pair_columns(vt_ref, group, j):
    low = lax.broadcasted_iota(jnp.int32, (T, 128), 1) < HD
    a = vt_ref[:, group + 2 * j : group + 2 * j + 1]
    b = vt_ref[:, group + 2 * j + 1 : group + 2 * j + 2]
    return jnp.where(low, a, b)


def pair_scalars(ref, j):
    low = lax.broadcasted_iota(jnp.int32, (1, 128), 1) < HD
    return jnp.where(low, ref[2 * j], ref[2 * j + 1])


def halves(v):
    low = (lax.broadcasted_iota(jnp.int32, (1, 128), 1) < HD).astype(v.dtype)
    return v * low, v * (1 - low)


def stack_rows(*refs):
    for i, ref in enumerate(refs[:-1]):
        refs[-1][i] = ref[...]


def join_cot(idx, here, left, right, far_a, far_b, own, send):
    c, x = idx[1], idx[2]
    half = T // 2
    for d, parts in (
        (0, ((here, 0, T),)),
        (1, ((left, 0, T),)),
        (2, ((far_a, 0, half), (far_b, half, half))),
        (3, ((right, 0, T),)),
    ):
        base = ((x - d + X) % X) * 256
        for k in range(2):
            to = pl.ds(pl.multiple_of(base + k * 128, 128), 128)
            at = pl.ds(pl.multiple_of(k * 256 + c * 128, 128), 128)
            other = pl.ds(pl.multiple_of(k * 256 + (1 - c) * 128, 128), 128)
            for ref, start, size in parts:
                own[start : start + size, to] = ref[:, at]
                send[start : start + size, to] = ref[:, other]


def head_column(ref):
    head = lax.broadcasted_iota(jnp.int32, (H, 1), 0)
    out = jnp.zeros((H, 1), F32)
    for h in range(H):
        out = jnp.where(head == h, ref[h], out)
    return out


def local_state(
    idx, lens, bias, dlog, raw_hbm, x_hbm, b_hbm, pay, vecs, vecst, raw, x, b, sems
):
    copies = [
        pltpu.make_async_copy(src, dst, sems.at[i])
        for i, (src, dst) in enumerate(((raw_hbm, raw), (x_hbm, x), (b_hbm, b)))
    ]
    for copy in copies:
        copy.start()
    base = (idx[0] * 2 + idx[1]) * T
    copies[0].wait()
    v = raw[...] + head_column(bias)
    dt = jnp.maximum(v, 0.0) + jnp.log1p(jnp.exp(-jnp.abs(v)))
    a = -jnp.exp(head_column(dlog)) * dt * LOG2E
    row = lax.broadcasted_iota(jnp.int32, (T, T), 0)
    col = lax.broadcasted_iota(jnp.int32, (T, T), 1)
    cum = nn(a, (row <= col).astype(F32), precision=HIGH)
    cumdt = cum - jnp.log(dt) * LOG2E
    pos = base + lax.broadcasted_iota(jnp.int32, (H, T), 1)
    seg = jnp.zeros((H, T), F32)
    last = jnp.float32(0)
    first = jnp.int32(0)
    for k in range(8):
        here = first >= base
        seg = seg + jnp.where(jnp.logical_and(here, pos >= first), 1.0, 0.0)
        last = last + jnp.where(jnp.logical_and(here, first < base + T), 1.0, 0.0)
        first = first + lens[0, k]
    end = jnp.where(seg == last, jnp.exp2(cum[:, T - 1 :] - cumdt), 0.0)
    reach = jnp.where(seg == 0.0, jnp.exp2(cum), 0.0)
    thru = jnp.where(last == 0.0, jnp.exp2(cum[:, T - 1 :]), 0.0)
    thru = jnp.broadcast_to(thru, (H, T))
    for at, value in (
        (CUM, cum),
        (CUMDT, cumdt),
        (REACH, reach),
        (END, end),
        (DT, dt),
        (SIG, jax.nn.sigmoid(v)),
        (THRU, thru),
        (SEG, seg),
    ):
        vecs[at : at + H, :] = value
    vecst[...] = vecs[...].T
    copies[1].wait()
    copies[2].wait()
    for j in range(H // 2):
        xs = x[:, j * 128 : (j + 1) * 128].astype(F32) * pair_columns(vecst, END, j)
        s = tn(xs.astype(BF16), b[...])
        pay[2 * j, 0:HD, :] = s[0:HD].astype(BF16)
        pay[2 * j + 1, 0:HD, :] = s[HD:].astype(BF16)
    hi = thru.astype(BF16)
    lo = (thru - hi.astype(F32)).astype(BF16)
    for h in range(H):
        pay[h, HD : HD + 8, :] = jnp.broadcast_to(hi[h : h + 1, 0:128].astype(F32), (8, 128)).astype(BF16)
        pay[h, HD + 8 :, :] = jnp.broadcast_to(lo[h : h + 1, 0:128].astype(F32), (8, 128)).astype(BF16)


def decay_of(block):
    tail = block[HD:, :].astype(F32)
    return tail[0:1] + tail[8:9]


def chip_state(idx, mine, theirs, out):
    c = idx[1]
    for k in range(8):
        m, t = mine[c * 8 + k], theirs[c * 8 + k]
        a = jnp.where(c == 0, m.astype(F32), t.astype(F32))
        b = jnp.where(c == 0, t.astype(F32), m.astype(F32))
        ta = a[HD : HD + 1] + a[HD + 8 : HD + 9]
        tb = b[HD : HD + 1] + b[HD + 8 : HD + 9]
        out[k, 0:HD, :] = (tb * a[0:HD] + b[0:HD]).astype(BF16)
        t = jnp.broadcast_to(ta * tb, (8, 128))
        hi = t.astype(BF16).astype(F32)
        out[k, HD:, :] = jnp.concatenate([hi, t - hi], axis=0).astype(BF16)


def merge_state(level, idx, mine, theirs, *refs):
    later = lax.rem(idx[0] // (1 << level), 2) == 1
    last = level == 2
    if level:
        before, past, ahead, refs = refs[0], refs[1], refs[2], refs[3:]
    entering, decays = refs[0], refs[1]
    for k in range(8):
        m, t = mine[k].astype(F32), theirs[k].astype(F32)
        tm, tt = m[HD : HD + 1] + m[HD + 8 : HD + 9], t[HD : HD + 1] + t[HD + 8 : HD + 9]
        m, t = m[0:HD], t[0:HD]
        tp = past[k : k + 1, :] if level else jnp.ones((1, N), F32)
        ts = ahead[k : k + 1, :] if level else jnp.ones((1, N), F32)
        new = jnp.where(later, tp, 0.0) * t
        entering[k] = before[k] + new if level else new
        decays[0, k : k + 1, :] = tm
        decays[1, k : k + 1, :] = tt
        decays[2, k : k + 1, :] = ts
        if not last:
            total, past_out, ahead_out = refs[2:]
            past_out[k : k + 1, :] = tp * jnp.where(later, tt, 1.0)
            ahead_out[k : k + 1, :] = ts * jnp.where(later, 1.0, tt)
            total[k, 0:HD, :] = jnp.where(later, tm * t + m, tt * m + t).astype(BF16)
            tail = jnp.broadcast_to(tm * tt, (8, N))
            hi = tail.astype(BF16).astype(F32)
            total[k, HD:, :] = jnp.concatenate([hi, tail - hi], axis=0).astype(BF16)


def chip_adjoint(idx, mine, theirs, pay_mine, pay_theirs, out):
    c = idx[1]
    for k in range(8):
        h = c * 8 + k
        m, t = mine[h].astype(F32), theirs[h].astype(F32)
        ta = jnp.where(c == 0, decay_of(pay_mine[h]), decay_of(pay_theirs[h]))
        a = jnp.where(c == 0, m, t)
        b = jnp.where(c == 0, t, m)
        out[k] = (a + ta * b).astype(BF16)


def merge_adjoint(level, idx, decays, mine, theirs, *refs):
    later = lax.rem(idx[0] // (1 << level), 2) == 1
    if level:
        before, refs = refs[0], refs[1:]
    for k in range(8):
        m, t = mine[k].astype(F32), theirs[k].astype(F32)
        tm, tt, ts = (decays[i, k : k + 1, :] for i in range(3))
        new = jnp.where(later, 0.0, ts) * t
        refs[0][k] = before[k] + new if level else new
        if level < 2:
            refs[1][k] = jnp.where(later, t + tt * m, m + tm * t).astype(BF16)


def place_states(idx, mine, theirs, local, pay, out, needs):
    c = idx[1]
    for k in range(8):
        for group, ref in ((c * 8, mine), (8 - c * 8, theirs)):
            h = group + k
            e = ref[k]
            past = decay_of(pay[h]) * e + local[h, 0:HD, :].astype(F32)
            at = pl.multiple_of(h * HD, HD)
            out[pl.ds(at, HD), :] = jnp.where(c == needs, past, e).astype(BF16)


def causal(vecs, vecst, transposed):
    row = lax.broadcasted_iota(jnp.int32, (T, T), 0)
    col = lax.broadcasted_iota(jnp.int32, (T, T), 1)
    order = row <= col if transposed else row >= col
    same = vecst[:, SEG : SEG + 1] == vecs[SEG : SEG + 1, :]
    return jnp.where(jnp.logical_and(order, same), 0.0, -1e30)


def inner_part(vecs, vecst, x, b, c, out):
    scores = nt(c[...], b[...])
    mask = causal(vecs, vecst, False)
    for j in range(H // 2):
        xs = halves(x[:, j * 128 : (j + 1) * 128])
        acc = None
        for k in range(2):
            h = 2 * j + k
            decay = jnp.exp2(
                vecst[:, CUM + h : CUM + h + 1] - vecs[CUMDT + h : CUMDT + h + 1, :] + mask
            )
            term = nn((decay * scores).astype(BF16), xs[k])
            acc = term if acc is None else acc + term
        out[:, j * 128 : (j + 1) * 128] = acc


def forward_out(idx, skip, vecst, x, c, inner, mine, theirs, pay, yy, rounded, state):
    place_states(idx, mine, theirs, pay, pay, state, 1)
    for j in range(H // 2):
        cols = slice(j * 128, (j + 1) * 128)
        carried = nt(c[...], state[j * 128 : (j + 1) * 128, :])
        y = inner[:, cols] + carried * pair_columns(vecst, REACH, j)
        yy[:, cols] = y
        rounded[:, cols] = (y + pair_scalars(skip, j) * x[:, cols].astype(F32)).astype(BF16)


def weight_part(idx, cot, cot_t, mine, theirs, *refs):
    y = idx[3]
    outs, buf = refs[:5], refs[5]
    p0, p1, p2a, p2b, p3 = outs
    for n in range(4):
        cols = slice(n * 256, (n + 1) * 256)
        r = tn(cot[...], mine[:, cols]) + tn(cot_t[...], theirs[:, cols])
        buf[:, :, :, cols] = r.reshape(Z, Y, 32, 256).astype(BF16)
    p0[...] = buf[:, y]
    p1[...] = buf[:, (y + 1) % Y]
    p2a[...] = buf[:, (y + 2) % Y, :, 0:512]
    p2b[...] = buf[:, (y + 2) % Y, :, 512:]
    p3[...] = buf[:, (y + 3) % Y]


def relay_rows(p1, p3, via_a, via_b, q1, q3):
    q1[:, :, 0:512] = (p1[:, :, 0:512].astype(F32) + via_a[...].astype(F32)).astype(BF16)
    q1[:, :, 512:] = p1[:, :, 512:]
    q3[:, :, 0:512] = p3[:, :, 0:512]
    q3[:, :, 512:] = (p3[:, :, 512:].astype(F32) + via_b[...].astype(F32)).astype(BF16)


def sum_rows(idx, p0, left, right, keep, send):
    bit = lax.rem(idx[0], 2)
    for j in range(4):
        for out, b in ((keep, bit), (send, 1 - bit)):
            k = 2 * j + b
            s = p0[k].astype(F32) + left[k].astype(F32) + right[k].astype(F32)
            out[j] = s.astype(out.dtype)


def spread_rows(idx, mine, theirs, own, one, two, three):
    j = idx[0] // 2
    own[...] = mine[j] + theirs[j].astype(F32)
    for k, out in enumerate((one, two, three)):
        i = (j + k + 1) % 4
        out[...] = (mine[i] + theirs[i].astype(F32)).astype(BF16)


def out_grad(idx, cot, cot_t, *refs):
    z, y = idx[0], idx[3]
    bundles, own, send, weights = refs[:8], refs[8], refs[9], refs[10]
    for i, d in enumerate((0, -1, 1, 2)):
        for group, steps in enumerate(STEPS):
            for k, step in enumerate(steps):
                weights[(z - step + Z) % Z, (y + d + Y) % Y] = bundles[2 * i + group][k]
    for n in range(4):
        cols = slice(n * 256, (n + 1) * 256)
        w = weights[:, :, :, cols].reshape(FC, 256)
        send[:, cols] = nn(cot_t[...], w).astype(BF16)
        own[:, cols] = nn(cot[...], w)


def local_adjoint(vecst, own, got, c, g, adj):
    for j in range(H // 2):
        cols = slice(j * 128, (j + 1) * 128)
        gj = (own[:, cols] + got[:, cols].astype(F32)).astype(BF16)
        g[:, cols] = gj
        gr = (gj.astype(F32) * pair_columns(vecst, REACH, j)).astype(BF16)
        s = tn(gr, c[...])
        adj[2 * j] = s[0:HD].astype(BF16)
        adj[2 * j + 1] = s[HD:].astype(BF16)


def inner_grads(vecs, vecst, x, b, c, g, state, dx, dc, db):
    scores = nt(b[...], c[...])
    mask = causal(vecs, vecst, True)
    dscores = jnp.zeros((T, T), F32)
    dstate = jnp.zeros((T, N), F32)
    for j in range(H // 2):
        cols = slice(j * 128, (j + 1) * 128)
        gj = g[:, cols]
        gs, xs = halves(gj), halves(x[:, cols])
        acc = None
        for k in range(2):
            h = 2 * j + k
            decay = jnp.exp2(
                vecs[CUM + h : CUM + h + 1, :] - vecst[:, CUMDT + h : CUMDT + h + 1] + mask
            )
            term = nn((decay * scores).astype(BF16), gs[k])
            acc = term if acc is None else acc + term
            dscores = dscores + nt(xs[k], gj) * decay
        dx[:, cols] = acc
        gr = (gj.astype(F32) * pair_columns(vecst, REACH, j)).astype(BF16)
        dstate = dstate + nn(gr, state[j * 128 : (j + 1) * 128, :])
    ds = dscores.astype(BF16)
    db[...] = nn(ds, c[...])
    dc[...] = tn(ds, b[...]) + dstate


def two_part(ones, v):
    hi = v.astype(BF16)
    lo = (v - hi.astype(F32)).astype(BF16)
    return nt(ones, hi) + nt(ones, lo)


def final_maps(idx, vecst, x, dbp, dc, mine, theirs, adjt, pay, maps, adj):
    place_states(idx, mine, theirs, adjt, pay, adj, 0)
    dbs = dbp[...]
    for j in range(H // 2):
        cols = slice(j * 128, (j + 1) * 128)
        xe = x[:, cols].astype(F32) * pair_columns(vecst, END, j)
        dbs = dbs + nn(xe.astype(BF16), adj[cols, :])
    maps[:, 0:N] = dbs.astype(BF16)
    maps[:, N:] = dc[...].astype(BF16)


def final_grads(
    skip, dlog, vecs, vecst, x, b, g, yy, dxm, state, adj, dx, dstep, flow, direct
):
    ends = []
    for j in range(H // 2):
        cols = slice(j * 128, (j + 1) * 128)
        rows = slice(j * 128, (j + 1) * 128)
        end = pair_columns(vecst, END, j)
        xj = x[:, cols].astype(F32)
        gj = g[:, cols].astype(F32)
        dxe = end * nt(b[...], adj[rows, :])
        dxx = dxm[:, cols] + dxe
        dx[:, cols] = (dxx + pair_scalars(skip, j) * gj).astype(BF16)
        prod = xj * dxx
        direct[:, cols] = prod
        flow[:, cols] = gj * yy[:, cols] - prod
        ends.append(jnp.sum(xj * dxe, axis=0, keepdims=True))
    head = lax.broadcasted_iota(jnp.int32, (H, W), 0)
    lane = lax.broadcasted_iota(jnp.int32, (H, W), 1)
    member = jnp.logical_and(lane >= head * HD, lane < head * HD + HD)
    ones = member.astype(BF16)
    dcum = two_part(ones, flow[...])
    ddt = two_part(ones, direct[...])
    total = jnp.sum(jnp.where(member, jnp.concatenate(ends, axis=1), 0.0), axis=1, keepdims=True)
    cross = jnp.sum(adj[...].astype(F32) * state[...].astype(F32), axis=1, keepdims=True)
    hi = cross.astype(BF16).astype(F32)
    cross = nn(ones, jnp.broadcast_to(hi, (W, 128)).astype(BF16)) + nn(
        ones, jnp.broadcast_to(cross - hi, (W, 128)).astype(BF16)
    )
    row = lax.broadcasted_iota(jnp.int32, (T, T), 0)
    col = lax.broadcasted_iota(jnp.int32, (T, T), 1)
    da = nn(dcum, (row >= col).astype(F32), precision=HIGH)
    da = da + total + vecs[THRU : THRU + H, 0:1] * cross[:, 0:1]
    ddt = ddt / vecs[DT : DT + H, :] - jnp.exp(head_column(dlog)) * da
    dstep[...] = ddt * vecs[SIG : SIG + H, :]


def last_sums(own, one, two, three, m0, m1, m2, m3, rows, db, dc):
    s = m0[...].astype(F32) + m1[...].astype(F32) + m2[...].astype(F32) + m3[...].astype(F32)
    db[...] = s[:, 0:N].astype(BF16)
    dc[...] = s[:, N:].astype(BF16)
    s = own[...] + one[...].astype(F32) + two[...].astype(F32) + three[...].astype(F32)
    rows[...] = s * (1.0 / 128.0)


def shift(v, axis, count, d):
    return lax.ppermute(v, axis, [(i, (i + d) % count) for i in range(count)])


def swap(v):
    return lax.ppermute(v, "core", [(0, 1), (1, 0)])


def facing(v, level):
    if level == 2:
        return lax.ppermute(v, "z", [(i, Z - 1 - i) for i in range(Z)])
    return lax.ppermute(v, "z", [(i, i ^ (1 << level)) for i in range(Z)])


def after(v, *others):
    return lax.optimization_barrier((v, others))[0]


def far_halves(left, right, axis, count):
    half = left.shape[0] // 2
    return shift(left[:half], axis, count, 1), shift(right[half:], axis, count, -1)


def on_device(
    ssm_input, input_map, output_map, step_raw, step_bias, decay_log, skip_gain, doc_lengths,
    out_weight, cotangent,
):
    x, b, c = ssm_input[0], input_map[0], output_map[0]
    raw = step_raw[0]
    idx = jnp.stack([lax.axis_index(a) for a in ("z", "core", "head", "fsdp")]).astype(jnp.int32)

    r1, l1 = shift(out_weight, "z", Z, 1), shift(out_weight, "z", Z, -1)
    cot_here = cotangent[0]
    cot_left, cot_right = shift(cot_here, "head", X, 1), shift(cot_here, "head", X, -1)

    pay, vecs, vecst = call(
        local_state,
        [((H, PAY, N), BF16), ((128, T), F32), ((T, 128), F32)],
        [idx, doc_lengths, step_bias, decay_log, raw, x, b],
        smem=(0, 1, 2, 3),
        hbm=(4, 5, 6),
        scratch=[
            pltpu.VMEM((H, T), F32),
            pltpu.VMEM((T, W), BF16),
            pltpu.VMEM((T, N), BF16),
            pltpu.SemaphoreType.DMA((3,)),
        ],
    )
    pay, r1, l1 = lax.optimization_barrier((pay, r1, l1))
    pay_t = swap(pay)
    r2, l2 = shift(r1, "z", Z, 1), shift(l1, "z", Z, -1)
    (block,) = call(chip_state, [((8, PAY, N), BF16)], [idx, pay, pay_t], smem=(0,))

    def join_states(level, block, got, carry):
        outs = [((8, HD, N), F32), ((3, 8, N), F32)]
        if level < 2:
            outs += [((8, PAY, N), BF16), ((8, N), F32), ((8, N), F32)]
        mine, decay, *rest = call(
            functools.partial(merge_state, level), outs, [idx, block, got, *carry], smem=(0,)
        )
        return mine, decay, rest

    got = facing(block, 0)
    r2, l2 = after((r2, l2), block)
    r3, l3 = shift(r2, "z", Z, 1), shift(l2, "z", Z, -1)
    (near,) = call(stack_rows, [((5, 32, W), BF16)], [out_weight, r1, l1, r2, l2])
    near_left, near_right = shift(near, "fsdp", Y, 1), shift(near, "fsdp", Y, -1)
    cot_far = far_halves(*after((cot_left, cot_right), near), "head", X)
    mine, decay0, rest = join_states(0, block, got, [])
    block, carry = rest[0], [mine, *rest[1:]]
    got = facing(block, 1)
    r4 = shift(r3, "z", Z, 1)
    (rest_rows,) = call(stack_rows, [((3, 32, W), BF16)], [r3, l3, r4])
    rest_left, rest_right = shift(rest_rows, "fsdp", Y, 1), shift(rest_rows, "fsdp", Y, -1)
    near_far = shift(near_left, "fsdp", Y, 1)
    got, rest_rows = lax.optimization_barrier((got, rest_rows))
    mine, decay1, rest = join_states(1, block, got, carry)
    block, carry = rest[0], [mine, *rest[1:]]
    got = facing(block, 2)
    rest_far = shift(rest_right, "fsdp", Y, -1)
    bundles = [
        near, rest_rows, near_left, rest_left, near_right, rest_right, near_far, rest_far,
    ]
    cot, cot_send = call(
        join_cot,
        [((T, FC), BF16)] * 2,
        [idx, cot_here, cot_left, cot_right, *cot_far],
        smem=(0,),
    )
    cot_t = swap(cot_send)
    (inner,) = call(inner_part, [((T, W), F32)], [vecs, vecst, x, b, c])
    mine, decay2, _ = join_states(2, block, got, carry)
    decays = [decay0, decay1, decay2]
    theirs = swap(mine)
    yy, rounded, state = call(
        forward_out,
        [((T, W), F32), ((T, W), BF16), ((W, N), BF16)],
        [idx, skip_gain, vecst, x, c, inner, mine, theirs, pay_t],
        smem=(0, 1),
    )

    rounded_t = swap(rounded)
    p0, p1, p2a, p2b, p3 = call(
        weight_part,
        [((Z, 32, W), BF16)] * 2 + [((Z, 32, W // 2), BF16)] * 2 + [((Z, 32, W), BF16)],
        [idx, cot, cot_t, rounded, rounded_t],
        smem=(0,),
        scratch=[pltpu.VMEM((Z, Y, 32, W), BF16)],
    )
    via_a, via_b = shift(p2a, "fsdp", Y, 1), shift(p2b, "fsdp", Y, -1)

    part, part_t = call(
        out_grad,
        [((T, W), F32), ((T, W), BF16)],
        [idx, cot, cot_t, *bundles],
        smem=(0,),
        scratch=[pltpu.VMEM((Z, Y, 32, W), BF16)],
    )
    g, adj = call(
        local_adjoint, [((T, W), BF16), ((H, HD, N), BF16)], [vecst, part, swap(part_t), c]
    )
    adj_t = swap(adj)
    (block,) = call(
        chip_adjoint, [((8, HD, N), BF16)], [idx, adj, adj_t, pay, pay_t], smem=(0,)
    )
    got = facing(block, 0)
    via_a, via_b = after((via_a, via_b), block)
    q1, q3 = call(
        relay_rows,
        [((Z, 32, W), BF16)] * 2,
        [p1, p3, via_a, via_b],
    )
    keep, send = call(
        sum_rows,
        [((4, 32, W), F32), ((4, 32, W), BF16)],
        [idx, p0, shift(q1, "fsdp", Y, 1), shift(q3, "fsdp", Y, -1)],
        smem=(0,),
    )
    paired = lax.ppermute(send, "z", [(i, i ^ 1) for i in range(Z)])
    own, *parts = call(
        spread_rows,
        [((32, W), F32)] + [((32, W), BF16)] * 3,
        [idx, keep, paired],
        smem=(0,),
    )
    parts = [shift(v, "z", Z, 2 * k + 2) for k, v in enumerate(parts)]

    dxm, dc, dbp = call(
        inner_grads,
        [((T, W), F32), ((T, N), F32), ((T, N), F32)],
        [vecs, vecst, x, b, c, g, state],
    )
    carry = []
    for level in range(3):
        outs = [((8, HD, N), F32)] + [((8, HD, N), BF16)] * (level < 2)
        mine, *rest = call(
            functools.partial(merge_adjoint, level),
            outs,
            [idx, decays[level], block, got, *carry],
            smem=(0,),
        )
        if rest:
            block, carry = rest[0], [mine]
            got = facing(block, level + 1)
            got = after(got, dxm)
    theirs = swap(mine)
    maps, adj = call(
        final_maps,
        [((T, 2 * N), BF16), ((W, N), BF16)],
        [idx, vecst, x, dbp, dc, mine, theirs, adj_t, pay_t],
        smem=(0,),
    )
    dx, dstep = call(
        final_grads,
        [((T, W), BF16), ((H, T), F32)],
        [skip_gain, decay_log, vecs, vecst, x, b, g, yy, dxm, state, adj],
        smem=(0, 1),
        scratch=[pltpu.VMEM((T, W), F32)] * 2,
    )
    weight_grad, db, dc = call(
        last_sums,
        [((32, W), F32), ((T, N), BF16), ((T, N), BF16)],
        [own, *parts, maps] + [shift(maps, "head", X, d) for d in (1, 2, 3)],
    )
    return dx[None], db[None], dc[None], dstep[None], weight_grad


def solution(mesh):
    inner = Mesh(mesh.devices.reshape(Z, 2, X, Y), ("z", "core", "head", "fsdp"))
    ctx = ("z", "core")
    features = ("z", "core", "fsdp")
    return jax.shard_map(
        on_device,
        mesh=inner,
        in_specs=(
            P("fsdp", ctx, "head"),
            P("fsdp", ctx, None),
            P("fsdp", ctx, None),
            P("fsdp", "head", ctx),
            P("head"),
            P("head"),
            P("head"),
            P("fsdp", None),
            P(features, "head"),
            P("fsdp", ctx, "head"),
        ),
        out_specs=(
            P("fsdp", ctx, "head"),
            P("fsdp", ctx, None),
            P("fsdp", ctx, None),
            P("fsdp", "head", ctx),
            P(features, "head"),
        ),
        check_vma=False,
    )
```

```python
import functools
import math

import jax
import jax.numpy as jnp
from jax import lax
from jax.experimental import pallas as pl
from jax.experimental.pallas import tpu as pltpu
from jax.sharding import Mesh, PartitionSpec as P

F32 = jnp.float32
BF16 = jnp.bfloat16
LOG2E = 1.4426950408889634
HIGH = lax.Precision.HIGHEST

T = 256
H = 16
HD = 64
N = 128
W = H * HD
FC = 1024
Z, Y, X = 8, 4, 4
STEPS = (0, 1, 7, 2, 6), (3, 5, 4)
PAY = HD + 16

WEIGHT = {
    "merge_state1": 8,
    "out_grad": 1,
    "weight_part": 0.1,
    "inner_grads": 0.6,
    "final_maps": 2,
    "forward_out": 2,
    "local_adjoint": 4,
    "merge_adjoint0": 0.1,
    "chip_state": 0.1,
    "merge_adjoint1": 2,
}

CUM, CUMDT, REACH, END, DT, SIG, THRU, SEG = range(0, 128, 16)


def nt(a, b, **kw):
    return lax.dot_general(a, b, (((1,), (1,)), ((), ())), preferred_element_type=F32, **kw)


def nn(a, b, **kw):
    return lax.dot_general(a, b, (((1,), (0,)), ((), ())), preferred_element_type=F32, **kw)


def tn(a, b, **kw):
    return lax.dot_general(a, b, (((0,), (0,)), ((), ())), preferred_element_type=F32, **kw)


def label_of(body):
    if hasattr(body, "func"):
        return body.func.__name__ + (str(body.args[0]) if isinstance(body.args[0], int) else "")
    return body.__name__


def call(body, outs, ins, smem=(), hbm=(), scratch=(), limit=40):
    shapes = [jax.ShapeDtypeStruct(s, d) for s, d in outs]
    specs = [
        pl.BlockSpec(
            memory_space=pltpu.SMEM if i in smem else pltpu.HBM if i in hbm else pltpu.VMEM
        )
        for i in range(len(ins))
    ]
    return pl.pallas_call(
        body,
        out_shape=shapes,
        in_specs=specs,
        out_specs=[pl.BlockSpec(memory_space=pltpu.VMEM)] * len(shapes),
        scratch_shapes=list(scratch),
        compiler_params=pltpu.CompilerParams(vmem_limit_bytes=limit << 20),
        cost_estimate=pl.CostEstimate(
            flops=int(WEIGHT.get(label_of(body), 0) * 1.15e9) + 1,
            bytes_accessed=1,
            transcendentals=0,
        ),
    )(*ins)


def pair_columns(vt_ref, group, j):
    low = lax.broadcasted_iota(jnp.int32, (T, 128), 1) < HD
    a = vt_ref[:, group + 2 * j : group + 2 * j + 1]
    b = vt_ref[:, group + 2 * j + 1 : group + 2 * j + 2]
    return jnp.where(low, a, b)


def pair_scalars(ref, j):
    low = lax.broadcasted_iota(jnp.int32, (1, 128), 1) < HD
    return jnp.where(low, ref[2 * j], ref[2 * j + 1])


def halves(v):
    low = (lax.broadcasted_iota(jnp.int32, (1, 128), 1) < HD).astype(v.dtype)
    return v * low, v * (1 - low)


def stack_rows(*refs):
    for i, ref in enumerate(refs[:-1]):
        refs[-1][i] = ref[...]


def join_cot(idx, here, left, right, far_a, far_b, own, send):
    c, x = idx[1], idx[2]
    half = T // 2
    for d, parts in (
        (0, ((here, 0, T),)),
        (1, ((left, 0, T),)),
        (2, ((far_a, 0, half), (far_b, half, half))),
        (3, ((right, 0, T),)),
    ):
        base = ((x - d + X) % X) * 256
        for k in range(2):
            to = pl.ds(pl.multiple_of(base + k * 128, 128), 128)
            at = pl.ds(pl.multiple_of(k * 256 + c * 128, 128), 128)
            other = pl.ds(pl.multiple_of(k * 256 + (1 - c) * 128, 128), 128)
            for ref, start, size in parts:
                own[start : start + size, to] = ref[:, at]
                send[start : start + size, to] = ref[:, other]


def head_column(ref):
    head = lax.broadcasted_iota(jnp.int32, (H, 1), 0)
    out = jnp.zeros((H, 1), F32)
    for h in range(H):
        out = jnp.where(head == h, ref[h], out)
    return out


def local_state(idx, lens, bias, dlog, raw, x, b, pay, vecs, vecst):
    base = (idx[0] * 2 + idx[1]) * T
    v = raw[...] + head_column(bias)
    dt = jnp.maximum(v, 0.0) + jnp.log1p(jnp.exp(-jnp.abs(v)))
    a = -jnp.exp(head_column(dlog)) * dt * LOG2E
    row = lax.broadcasted_iota(jnp.int32, (T, T), 0)
    col = lax.broadcasted_iota(jnp.int32, (T, T), 1)
    cum = nn(a, (row <= col).astype(F32), precision=HIGH)
    cumdt = cum - jnp.log(dt) * LOG2E
    pos = base + lax.broadcasted_iota(jnp.int32, (H, T), 1)
    seg = jnp.zeros((H, T), F32)
    last = jnp.float32(0)
    first = jnp.int32(0)
    for k in range(8):
        here = first >= base
        seg = seg + jnp.where(jnp.logical_and(here, pos >= first), 1.0, 0.0)
        last = last + jnp.where(jnp.logical_and(here, first < base + T), 1.0, 0.0)
        first = first + lens[0, k]
    end = jnp.where(seg == last, jnp.exp2(cum[:, T - 1 :] - cumdt), 0.0)
    reach = jnp.where(seg == 0.0, jnp.exp2(cum), 0.0)
    thru = jnp.where(last == 0.0, jnp.exp2(cum[:, T - 1 :]), 0.0)
    thru = jnp.broadcast_to(thru, (H, T))
    for at, value in (
        (CUM, cum),
        (CUMDT, cumdt),
        (REACH, reach),
        (END, end),
        (DT, dt),
        (SIG, jax.nn.sigmoid(v)),
        (THRU, thru),
        (SEG, seg),
    ):
        vecs[at : at + H, :] = value
    vecst[...] = vecs[...].T
    for j in range(H // 2):
        xs = x[:, j * 128 : (j + 1) * 128].astype(F32) * pair_columns(vecst, END, j)
        s = tn(xs.astype(BF16), b[...])
        pay[2 * j, 0:HD, :] = s[0:HD].astype(BF16)
        pay[2 * j + 1, 0:HD, :] = s[HD:].astype(BF16)
    hi = thru.astype(BF16)
    lo = (thru - hi.astype(F32)).astype(BF16)
    for h in range(H):
        pay[h, HD : HD + 8, :] = jnp.broadcast_to(hi[h : h + 1, 0:128].astype(F32), (8, 128)).astype(BF16)
        pay[h, HD + 8 :, :] = jnp.broadcast_to(lo[h : h + 1, 0:128].astype(F32), (8, 128)).astype(BF16)


def decay_of(block):
    tail = block[HD:, :].astype(F32)
    return tail[0:1] + tail[8:9]


def chip_state(idx, mine, theirs, out):
    c = idx[1]
    for k in range(8):
        m, t = mine[c * 8 + k], theirs[c * 8 + k]
        a = jnp.where(c == 0, m.astype(F32), t.astype(F32))
        b = jnp.where(c == 0, t.astype(F32), m.astype(F32))
        ta = a[HD : HD + 1] + a[HD + 8 : HD + 9]
        tb = b[HD : HD + 1] + b[HD + 8 : HD + 9]
        out[k, 0:HD, :] = (tb * a[0:HD] + b[0:HD]).astype(BF16)
        t = jnp.broadcast_to(ta * tb, (8, 128))
        hi = t.astype(BF16).astype(F32)
        out[k, HD:, :] = jnp.concatenate([hi, t - hi], axis=0).astype(BF16)


def merge_state(level, idx, mine, theirs, *refs):
    later = lax.rem(idx[0] // (1 << level), 2) == 1
    last = level == 2
    if level:
        before, past, ahead, refs = refs[0], refs[1], refs[2], refs[3:]
    entering, decays = refs[0], refs[1]
    for k in range(8):
        m, t = mine[k].astype(F32), theirs[k].astype(F32)
        tm, tt = m[HD : HD + 1] + m[HD + 8 : HD + 9], t[HD : HD + 1] + t[HD + 8 : HD + 9]
        m, t = m[0:HD], t[0:HD]
        tp = past[k : k + 1, :] if level else jnp.ones((1, N), F32)
        ts = ahead[k : k + 1, :] if level else jnp.ones((1, N), F32)
        new = jnp.where(later, tp, 0.0) * t
        entering[k] = before[k] + new if level else new
        decays[0, k : k + 1, :] = tm
        decays[1, k : k + 1, :] = tt
        decays[2, k : k + 1, :] = ts
        if not last:
            total, past_out, ahead_out = refs[2:]
            past_out[k : k + 1, :] = tp * jnp.where(later, tt, 1.0)
            ahead_out[k : k + 1, :] = ts * jnp.where(later, 1.0, tt)
            total[k, 0:HD, :] = jnp.where(later, tm * t + m, tt * m + t).astype(BF16)
            tail = jnp.broadcast_to(tm * tt, (8, N))
            hi = tail.astype(BF16).astype(F32)
            total[k, HD:, :] = jnp.concatenate([hi, tail - hi], axis=0).astype(BF16)


def chip_adjoint(idx, mine, theirs, pay_mine, pay_theirs, out):
    c = idx[1]
    for k in range(8):
        h = c * 8 + k
        m, t = mine[h].astype(F32), theirs[h].astype(F32)
        ta = jnp.where(c == 0, decay_of(pay_mine[h]), decay_of(pay_theirs[h]))
        a = jnp.where(c == 0, m, t)
        b = jnp.where(c == 0, t, m)
        out[k] = (a + ta * b).astype(BF16)


def merge_adjoint(level, idx, decays, mine, theirs, *refs):
    later = lax.rem(idx[0] // (1 << level), 2) == 1
    if level:
        before, refs = refs[0], refs[1:]
    for k in range(8):
        m, t = mine[k].astype(F32), theirs[k].astype(F32)
        tm, tt, ts = (decays[i, k : k + 1, :] for i in range(3))
        new = jnp.where(later, 0.0, ts) * t
        refs[0][k] = before[k] + new if level else new
        if level < 2:
            refs[1][k] = jnp.where(later, t + tt * m, m + tm * t).astype(BF16)


def place_states(idx, mine, theirs, local, pay, out, needs):
    c = idx[1]
    for k in range(8):
        for group, ref in ((c * 8, mine), (8 - c * 8, theirs)):
            h = group + k
            e = ref[k]
            past = decay_of(pay[h]) * e + local[h, 0:HD, :].astype(F32)
            at = pl.multiple_of(h * HD, HD)
            out[pl.ds(at, HD), :] = jnp.where(c == needs, past, e).astype(BF16)


def causal(vecs, vecst, transposed):
    row = lax.broadcasted_iota(jnp.int32, (T, T), 0)
    col = lax.broadcasted_iota(jnp.int32, (T, T), 1)
    order = row <= col if transposed else row >= col
    same = vecst[:, SEG : SEG + 1] == vecs[SEG : SEG + 1, :]
    return jnp.where(jnp.logical_and(order, same), 0.0, -1e30)


def inner_part(vecs, vecst, x, b, c, out):
    scores = nt(c[...], b[...])
    mask = causal(vecs, vecst, False)
    for j in range(H // 2):
        xs = halves(x[:, j * 128 : (j + 1) * 128])
        acc = None
        for k in range(2):
            h = 2 * j + k
            decay = jnp.exp2(
                vecst[:, CUM + h : CUM + h + 1] - vecs[CUMDT + h : CUMDT + h + 1, :] + mask
            )
            term = nn((decay * scores).astype(BF16), xs[k])
            acc = term if acc is None else acc + term
        out[:, j * 128 : (j + 1) * 128] = acc


def forward_out(idx, skip, vecst, x, c, inner, mine, theirs, pay, yy, rounded, state):
    place_states(idx, mine, theirs, pay, pay, state, 1)
    for j in range(H // 2):
        cols = slice(j * 128, (j + 1) * 128)
        carried = nt(c[...], state[j * 128 : (j + 1) * 128, :])
        y = inner[:, cols] + carried * pair_columns(vecst, REACH, j)
        yy[:, cols] = y
        rounded[:, cols] = (y + pair_scalars(skip, j) * x[:, cols].astype(F32)).astype(BF16)


def weight_part(idx, cot, cot_t, mine, theirs, *refs):
    y = idx[3]
    outs, buf = refs[:5], refs[5]
    p0, p1, p2a, p2b, p3 = outs
    for n in range(4):
        cols = slice(n * 256, (n + 1) * 256)
        r = tn(cot[...], mine[:, cols]) + tn(cot_t[...], theirs[:, cols])
        buf[:, :, :, cols] = r.reshape(Z, Y, 32, 256).astype(BF16)
    p0[...] = buf[:, y]
    p1[...] = buf[:, (y + 1) % Y]
    p2a[...] = buf[:, (y + 2) % Y, :, 0:512]
    p2b[...] = buf[:, (y + 2) % Y, :, 512:]
    p3[...] = buf[:, (y + 3) % Y]


def relay_rows(p1, p3, via_a, via_b, q1, q3):
    q1[:, :, 0:512] = (p1[:, :, 0:512].astype(F32) + via_a[...].astype(F32)).astype(BF16)
    q1[:, :, 512:] = p1[:, :, 512:]
    q3[:, :, 0:512] = p3[:, :, 0:512]
    q3[:, :, 512:] = (p3[:, :, 512:].astype(F32) + via_b[...].astype(F32)).astype(BF16)


def sum_rows(idx, p0, left, right, keep, send):
    bit = lax.rem(idx[0], 2)
    for j in range(4):
        for out, b in ((keep, bit), (send, 1 - bit)):
            k = 2 * j + b
            s = p0[k].astype(F32) + left[k].astype(F32) + right[k].astype(F32)
            out[j] = s.astype(out.dtype)


def spread_rows(idx, mine, theirs, own, one, two, three):
    j = idx[0] // 2
    own[...] = mine[j] + theirs[j].astype(F32)
    for k, out in enumerate((one, two, three)):
        i = (j + k + 1) % 4
        out[...] = (mine[i] + theirs[i].astype(F32)).astype(BF16)


def out_grad(idx, cot, cot_t, *refs):
    z, y = idx[0], idx[3]
    bundles, own, send, weights = refs[:8], refs[8], refs[9], refs[10]
    for i, d in enumerate((0, -1, 1, 2)):
        for group, steps in enumerate(STEPS):
            for k, step in enumerate(steps):
                weights[(z - step + Z) % Z, (y + d + Y) % Y] = bundles[2 * i + group][k]
    for n in range(4):
        cols = slice(n * 256, (n + 1) * 256)
        w = weights[:, :, :, cols].reshape(FC, 256)
        send[:, cols] = nn(cot_t[...], w).astype(BF16)
        own[:, cols] = nn(cot[...], w)


def local_adjoint(vecst, own, got, c, g, adj):
    for j in range(H // 2):
        cols = slice(j * 128, (j + 1) * 128)
        gj = (own[:, cols] + got[:, cols].astype(F32)).astype(BF16)
        g[:, cols] = gj
        gr = (gj.astype(F32) * pair_columns(vecst, REACH, j)).astype(BF16)
        s = tn(gr, c[...])
        adj[2 * j] = s[0:HD].astype(BF16)
        adj[2 * j + 1] = s[HD:].astype(BF16)


def inner_grads(vecs, vecst, x, b, c, g, state, dx, dc, db):
    scores = nt(b[...], c[...])
    mask = causal(vecs, vecst, True)
    dscores = jnp.zeros((T, T), F32)
    dstate = jnp.zeros((T, N), F32)
    for j in range(H // 2):
        cols = slice(j * 128, (j + 1) * 128)
        gj = g[:, cols]
        gs, xs = halves(gj), halves(x[:, cols])
        acc = None
        for k in range(2):
            h = 2 * j + k
            decay = jnp.exp2(
                vecs[CUM + h : CUM + h + 1, :] - vecst[:, CUMDT + h : CUMDT + h + 1] + mask
            )
            term = nn((decay * scores).astype(BF16), gs[k])
            acc = term if acc is None else acc + term
            dscores = dscores + nt(xs[k], gj) * decay
        dx[:, cols] = acc
        gr = (gj.astype(F32) * pair_columns(vecst, REACH, j)).astype(BF16)
        dstate = dstate + nn(gr, state[j * 128 : (j + 1) * 128, :])
    ds = dscores.astype(BF16)
    db[...] = nn(ds, c[...])
    dc[...] = tn(ds, b[...]) + dstate


def two_part(ones, v):
    hi = v.astype(BF16)
    lo = (v - hi.astype(F32)).astype(BF16)
    return nt(ones, hi) + nt(ones, lo)


def final_maps(idx, vecst, x, dbp, dc, mine, theirs, adjt, pay, maps, adj):
    place_states(idx, mine, theirs, adjt, pay, adj, 0)
    dbs = dbp[...]
    for j in range(H // 2):
        cols = slice(j * 128, (j + 1) * 128)
        xe = x[:, cols].astype(F32) * pair_columns(vecst, END, j)
        dbs = dbs + nn(xe.astype(BF16), adj[cols, :])
    maps[:, 0:N] = dbs.astype(BF16)
    maps[:, N:] = dc[...].astype(BF16)


def final_grads(
    skip, dlog, vecs, vecst, x, b, g, yy, dxm, state, adj, dx, dstep, flow, direct
):
    ends = []
    for j in range(H // 2):
        cols = slice(j * 128, (j + 1) * 128)
        rows = slice(j * 128, (j + 1) * 128)
        end = pair_columns(vecst, END, j)
        xj = x[:, cols].astype(F32)
        gj = g[:, cols].astype(F32)
        dxe = end * nt(b[...], adj[rows, :])
        dxx = dxm[:, cols] + dxe
        dx[:, cols] = (dxx + pair_scalars(skip, j) * gj).astype(BF16)
        prod = xj * dxx
        direct[:, cols] = prod
        flow[:, cols] = gj * yy[:, cols] - prod
        ends.append(jnp.sum(xj * dxe, axis=0, keepdims=True))
    head = lax.broadcasted_iota(jnp.int32, (H, W), 0)
    lane = lax.broadcasted_iota(jnp.int32, (H, W), 1)
    member = jnp.logical_and(lane >= head * HD, lane < head * HD + HD)
    ones = member.astype(BF16)
    dcum = two_part(ones, flow[...])
    ddt = two_part(ones, direct[...])
    total = jnp.sum(jnp.where(member, jnp.concatenate(ends, axis=1), 0.0), axis=1, keepdims=True)
    cross = jnp.sum(adj[...].astype(F32) * state[...].astype(F32), axis=1, keepdims=True)
    hi = cross.astype(BF16).astype(F32)
    cross = nn(ones, jnp.broadcast_to(hi, (W, 128)).astype(BF16)) + nn(
        ones, jnp.broadcast_to(cross - hi, (W, 128)).astype(BF16)
    )
    row = lax.broadcasted_iota(jnp.int32, (T, T), 0)
    col = lax.broadcasted_iota(jnp.int32, (T, T), 1)
    da = nn(dcum, (row >= col).astype(F32), precision=HIGH)
    da = da + total + vecs[THRU : THRU + H, 0:1] * cross[:, 0:1]
    ddt = ddt / vecs[DT : DT + H, :] - jnp.exp(head_column(dlog)) * da
    dstep[...] = ddt * vecs[SIG : SIG + H, :]


def last_sums(own, one, two, three, m0, m1, m2, m3, rows, db, dc):
    s = m0[...].astype(F32) + m1[...].astype(F32) + m2[...].astype(F32) + m3[...].astype(F32)
    db[...] = s[:, 0:N].astype(BF16)
    dc[...] = s[:, N:].astype(BF16)
    s = own[...] + one[...].astype(F32) + two[...].astype(F32) + three[...].astype(F32)
    rows[...] = s * (1.0 / 128.0)


def shift(v, axis, count, d):
    return lax.ppermute(v, axis, [(i, (i + d) % count) for i in range(count)])


def swap(v):
    return lax.ppermute(v, "core", [(0, 1), (1, 0)])


def facing(v, level):
    if level == 2:
        return lax.ppermute(v, "z", [(i, Z - 1 - i) for i in range(Z)])
    return lax.ppermute(v, "z", [(i, i ^ (1 << level)) for i in range(Z)])


def after(v, *others):
    return lax.optimization_barrier((v, others))[0]


def far_halves(left, right, axis, count):
    half = left.shape[0] // 2
    return shift(left[:half], axis, count, 1), shift(right[half:], axis, count, -1)


def on_device(
    ssm_input, input_map, output_map, step_raw, step_bias, decay_log, skip_gain, doc_lengths,
    out_weight, cotangent,
):
    x, b, c = ssm_input[0], input_map[0], output_map[0]
    raw = step_raw[0]
    idx = jnp.stack([lax.axis_index(a) for a in ("z", "core", "head", "fsdp")]).astype(jnp.int32)

    r1, l1 = shift(out_weight, "z", Z, 1), shift(out_weight, "z", Z, -1)
    cot_here = cotangent[0]
    cot_left, cot_right = shift(cot_here, "head", X, 1), shift(cot_here, "head", X, -1)

    pay, vecs, vecst = call(
        local_state,
        [((H, PAY, N), BF16), ((128, T), F32), ((T, 128), F32)],
        [idx, doc_lengths, step_bias, decay_log, raw, x, b],
        smem=(0, 1, 2, 3),
    )
    pay, r1, l1 = lax.optimization_barrier((pay, r1, l1))
    pay_t = swap(pay)
    r2, l2 = shift(r1, "z", Z, 1), shift(l1, "z", Z, -1)
    (block,) = call(chip_state, [((8, PAY, N), BF16)], [idx, pay, pay_t], smem=(0,))

    def join_states(level, block, got, carry):
        outs = [((8, HD, N), F32), ((3, 8, N), F32)]
        if level < 2:
            outs += [((8, PAY, N), BF16), ((8, N), F32), ((8, N), F32)]
        mine, decay, *rest = call(
            functools.partial(merge_state, level), outs, [idx, block, got, *carry], smem=(0,)
        )
        return mine, decay, rest

    got = facing(block, 0)
    r2, l2 = after((r2, l2), block)
    r3, l3 = shift(r2, "z", Z, 1), shift(l2, "z", Z, -1)
    (near,) = call(stack_rows, [((5, 32, W), BF16)], [out_weight, r1, l1, r2, l2])
    near_left, near_right = shift(near, "fsdp", Y, 1), shift(near, "fsdp", Y, -1)
    cot_far = far_halves(*after((cot_left, cot_right), near), "head", X)
    mine, decay0, rest = join_states(0, block, got, [])
    block, carry = rest[0], [mine, *rest[1:]]
    got = facing(block, 1)
    r4 = shift(r3, "z", Z, 1)
    (rest_rows,) = call(stack_rows, [((3, 32, W), BF16)], [r3, l3, r4])
    rest_left, rest_right = shift(rest_rows, "fsdp", Y, 1), shift(rest_rows, "fsdp", Y, -1)
    near_far = shift(near_left, "fsdp", Y, 1)
    got, rest_rows = lax.optimization_barrier((got, rest_rows))
    mine, decay1, rest = join_states(1, block, got, carry)
    block, carry = rest[0], [mine, *rest[1:]]
    got = facing(block, 2)
    rest_far = shift(rest_right, "fsdp", Y, -1)
    bundles = [
        near, rest_rows, near_left, rest_left, near_right, rest_right, near_far, rest_far,
    ]
    cot, cot_send = call(
        join_cot,
        [((T, FC), BF16)] * 2,
        [idx, cot_here, cot_left, cot_right, *cot_far],
        smem=(0,),
    )
    cot_t = swap(cot_send)
    (inner,) = call(inner_part, [((T, W), F32)], [vecs, vecst, x, b, c])
    mine, decay2, _ = join_states(2, block, got, carry)
    decays = [decay0, decay1, decay2]
    theirs = swap(mine)
    yy, rounded, state = call(
        forward_out,
        [((T, W), F32), ((T, W), BF16), ((W, N), BF16)],
        [idx, skip_gain, vecst, x, c, inner, mine, theirs, pay_t],
        smem=(0, 1),
    )

    rounded_t = swap(rounded)
    p0, p1, p2a, p2b, p3 = call(
        weight_part,
        [((Z, 32, W), BF16)] * 2 + [((Z, 32, W // 2), BF16)] * 2 + [((Z, 32, W), BF16)],
        [idx, cot, cot_t, rounded, rounded_t],
        smem=(0,),
        scratch=[pltpu.VMEM((Z, Y, 32, W), BF16)],
    )
    via_a, via_b = shift(p2a, "fsdp", Y, 1), shift(p2b, "fsdp", Y, -1)

    part, part_t = call(
        out_grad,
        [((T, W), F32), ((T, W), BF16)],
        [idx, cot, cot_t, *bundles],
        smem=(0,),
        scratch=[pltpu.VMEM((Z, Y, 32, W), BF16)],
    )
    g, adj = call(
        local_adjoint, [((T, W), BF16), ((H, HD, N), BF16)], [vecst, part, swap(part_t), c]
    )
    adj_t = swap(adj)
    (block,) = call(
        chip_adjoint, [((8, HD, N), BF16)], [idx, adj, adj_t, pay, pay_t], smem=(0,)
    )
    got = facing(block, 0)
    via_a, via_b = after((via_a, via_b), block)
    q1, q3 = call(
        relay_rows,
        [((Z, 32, W), BF16)] * 2,
        [p1, p3, via_a, via_b],
    )
    keep, send = call(
        sum_rows,
        [((4, 32, W), F32), ((4, 32, W), BF16)],
        [idx, p0, shift(q1, "fsdp", Y, 1), shift(q3, "fsdp", Y, -1)],
        smem=(0,),
    )
    paired = lax.ppermute(send, "z", [(i, i ^ 1) for i in range(Z)])
    own, *parts = call(
        spread_rows,
        [((32, W), F32)] + [((32, W), BF16)] * 3,
        [idx, keep, paired],
        smem=(0,),
    )
    parts = [shift(v, "z", Z, 2 * k + 2) for k, v in enumerate(parts)]

    dxm, dc, dbp = call(
        inner_grads,
        [((T, W), F32), ((T, N), F32), ((T, N), F32)],
        [vecs, vecst, x, b, c, g, state],
    )
    carry = []
    for level in range(3):
        outs = [((8, HD, N), F32)] + [((8, HD, N), BF16)] * (level < 2)
        mine, *rest = call(
            functools.partial(merge_adjoint, level),
            outs,
            [idx, decays[level], block, got, *carry],
            smem=(0,),
        )
        if rest:
            block, carry = rest[0], [mine]
            got = facing(block, level + 1)
            got = after(got, dxm)
    theirs = swap(mine)
    maps, adj = call(
        final_maps,
        [((T, 2 * N), BF16), ((W, N), BF16)],
        [idx, vecst, x, dbp, dc, mine, theirs, adj_t, pay_t],
        smem=(0,),
    )
    dx, dstep = call(
        final_grads,
        [((T, W), BF16), ((H, T), F32)],
        [skip_gain, decay_log, vecs, vecst, x, b, g, yy, dxm, state, adj],
        smem=(0, 1),
        scratch=[pltpu.VMEM((T, W), F32)] * 2,
    )
    weight_grad, db, dc = call(
        last_sums,
        [((32, W), F32), ((T, N), BF16), ((T, N), BF16)],
        [own, *parts, maps] + [shift(maps, "head", X, d) for d in (1, 2, 3)],
    )
    return dx[None], db[None], dc[None], dstep[None], weight_grad


def solution(mesh):
    inner = Mesh(mesh.devices.reshape(Z, 2, X, Y), ("z", "core", "head", "fsdp"))
    ctx = ("z", "core")
    features = ("z", "core", "fsdp")
    return jax.shard_map(
        on_device,
        mesh=inner,
        in_specs=(
            P("fsdp", ctx, "head"),
            P("fsdp", ctx, None),
            P("fsdp", ctx, None),
            P("fsdp", "head", ctx),
            P("head"),
            P("head"),
            P("head"),
            P("fsdp", None),
            P(features, "head"),
            P("fsdp", ctx, "head"),
        ),
        out_specs=(
            P("fsdp", ctx, "head"),
            P("fsdp", ctx, None),
            P("fsdp", ctx, None),
            P("fsdp", "head", ctx),
            P(features, "head"),
        ),
        check_vma=False,
    )
```
